512 devices in a mesh: ray: 16 (over y, x_hi, core), cuts: 32 (over x_lo, z).
Axes of the slice: x: 4 (x_hi: 2, x_lo: 2; x = x_hi * 2 + x_lo), y: 4, z: 16, core: 2. Of those that a mesh axis runs over, the one named last changes fastest.
Arguments:
- initial: float32 [64, 64, 4096], P('cuts', 'ray'), may hold values from 0.5 to 1.5
- measured: float32 [16, 32, 64, 4096], P('ray', None, 'cuts'), may hold values from 38.4 to 115.2
- order: int32 [16], replicated, may hold values from 0 to 15, each once
- angle_index: int32 [16, 32], replicated, may hold values from 0 to 2999
Outputs:
- reconstruction: float32 [64, 64, 4096], P('cuts', 'ray')
The draws below stay inside these ranges and needn't reach their ends.
Inputs may be any that keep to these rules, and one draw needn't show every extreme that they name: Each stored subset appears once; the first 2 entries are the subsets run, in order, and stored subset j is held by index j of ray.
All inputs are finite; a program needn't handle non-finite values.
Results may differ from the reference program's by a relative error of at most 0.0003.
Values sent between devices are 32-bit elements; how exact they have to be, the bound alone decides.
A program may use at most 64 MiB of HBM per device.

```python
import jax
import jax.numpy as jnp
from jax import lax

W = 4096
ANG = 32
SUBSETS = 2
NANG = 3000
TV_ITERS = 2
NR = 64
SLICES = 64
STORED = 16


def set_ends(result, stream_key, least, high):
    longest = result.shape.index(max(result.shape))
    spots = []
    for shift in (0, 1):
        where = [jax.random.randint(jax.random.fold_in(stream_key, axis), (), 0, length) for axis, length in enumerate(result.shape)]
        where[longest] = (where[longest] + shift) % result.shape[longest]
        spots.append(tuple(where))
    return result.at[spots[0]].set(least).at[spots[1]].set(high)


def block_scale(own_key, dims, cuts, least, high):
    factor_of, own = 1.0, jax.random.fold_in(own_key, 6)
    for axis_at, shards_of in cuts:
        heights = jnp.exp(jax.random.uniform(jax.random.fold_in(own, axis_at), (shards_of,), jnp.float32, least / len(cuts), high / len(cuts)))
        factor_of = factor_of * jnp.repeat(heights, dims[axis_at] // shards_of).reshape([-1 if axis == axis_at else 1 for axis in range(len(dims))])
    return factor_of


def setup_inputs(seed: int = 0) -> dict:
    seeds = jax.random.split(jax.random.key(seed), 5)
    return {
        "initial": jnp.clip(0.5 + 1.0 * jax.random.uniform(seeds[0], (SLICES, NR, W), jnp.float32) ** block_scale(seeds[0], (SLICES, NR, W), ((0, 32), (1, 16)), -0.2, 0.2), 0.5, 1.5),
        "measured": jnp.clip(38.4 + 76.799995 * jax.random.uniform(seeds[1], (STORED, ANG, SLICES, W), jnp.float32) ** block_scale(seeds[1], (STORED, ANG, SLICES, W), ((0, 16), (2, 32)), -0.2, 0.2), 38.4, 115.2),
        "order": jax.random.permutation(seeds[2], STORED).astype(jnp.int32),
        "angle_index": set_ends(jax.random.randint(seeds[3], (STORED, ANG), 0, NANG), jax.random.fold_in(seeds[3], 1), 0, NANG - 1).astype(jnp.int32),
    }


TV_STEP = 0.05
TV_EPS = 0.5

def geometry(angle_row):
    slopes = -1.0 + (2.0 * angle_row.astype(jnp.float32) + 1.0) / NANG
    row_pos = jnp.arange(NR, dtype=jnp.int32).astype(jnp.float32) - (NR - 1) / 2.0
    spread = slopes[:, None] * row_pos[None, :]
    floor_part = jnp.floor(spread)
    return (floor_part.astype(jnp.int32), spread - floor_part)

def project(current, shifts, fraction):
    margin = NR // 2 + 2
    padded = jnp.pad(current, ((0, 0), (0, 0), (margin, margin)))
    columns = jnp.arange(W, dtype=jnp.int32)

    def one_angle(pieces):
        shift_row, frac_row = pieces
        lead_index = columns[None, :] - shift_row[:, None] + margin
        lead_index = jnp.broadcast_to(lead_index[None], current.shape)
        near_tap = jnp.take_along_axis(padded, lead_index, axis=2)
        far_tap = jnp.take_along_axis(padded, lead_index - 1, axis=2)
        weight = frac_row[None, :, None]
        return lax.optimization_barrier(jnp.sum((1.0 - weight) * near_tap + weight * far_tap, axis=1))
    return lax.map(one_angle, (shifts, fraction))

def back_project(residual, shifts, fraction, shape):
    margin = NR // 2 + 2
    padded = jnp.pad(residual, ((0, 0), (0, 0), (margin, margin)))
    columns = jnp.arange(W, dtype=jnp.int32)

    def add_angle(summed, pieces):
        sino_plane, shift_row, frac_row = pieces
        lead_index = columns[None, :] + shift_row[:, None] + margin
        near_tap = jnp.take(sino_plane, lead_index, axis=1)
        far_tap = jnp.take(sino_plane, lead_index + 1, axis=1)
        weight = frac_row[None, :, None]
        return (summed + (1.0 - weight) * near_tap + weight * far_tap, None)
    summed, _ = lax.scan(add_angle, jnp.zeros(shape, jnp.float32), (padded, shifts, fraction))
    return summed

def tv_step(current):
    step_s = jnp.concatenate([current[1:] - current[:-1], jnp.zeros_like(current[:1])], axis=0)
    step_r = jnp.concatenate([current[:, 1:] - current[:, :-1], jnp.zeros_like(current[:, :1])], axis=1)
    step_c = jnp.concatenate([current[:, :, 1:] - current[:, :, :-1], jnp.zeros_like(current[:, :, :1])], axis=2)
    magnitude = jnp.sqrt(step_s * step_s + step_r * step_r + step_c * step_c + TV_EPS * TV_EPS)
    flow_s = step_s / magnitude
    flow_r = step_r / magnitude
    flow_c = step_c / magnitude
    spread = flow_s - jnp.concatenate([jnp.zeros_like(flow_s[:1]), flow_s[:-1]], axis=0)
    spread = spread + flow_r - jnp.concatenate([jnp.zeros_like(flow_r[:, :1]), flow_r[:, :-1]], axis=1)
    spread = spread + flow_c - jnp.concatenate([jnp.zeros_like(flow_c[:, :, :1]), flow_c[:, :, :-1]], axis=2)
    return current + TV_STEP * spread

def reference(initial, measured, order, angle_index):
    current = initial
    for subset in range(SUBSETS):
        subset_slot = order[subset]
        shifts, fraction = geometry(angle_index[subset_slot])
        forward = project(current, shifts, fraction)
        residual = measured[subset_slot] - forward
        current = current + back_project(residual, shifts, fraction, current.shape) / (NR * ANG)
        for tv_turn in range(TV_ITERS):
            current = tv_step(current)
    return current
```

```python
import functools

import jax
import jax.numpy as jnp
from jax import lax
from jax.experimental import pallas as pl
from jax.experimental.pallas import tpu as pltpu
from jax.sharding import PartitionSpec as P

SUBSETS = 2
NANG = 3000
TV_ITERS = 2
TV_STEP = 0.05
TV_EPS = 0.5
MESH = pl.DeviceIdType.MESH
LANE = 128


def split(value):
    high = value.astype(jnp.bfloat16)
    return high, (value - high.astype(jnp.float32)).astype(jnp.bfloat16)


def dot3(left_hi, left_lo, right):
    right_hi, right_lo = split(right)
    dot = functools.partial(jnp.dot, preferred_element_type=jnp.float32)
    return dot(left_hi, right_hi) + dot(left_lo, right_hi) + dot(left_hi, right_lo)


def kernel(
    rays, cuts,
    init_ref, meas_ref, order_ref, angle_ref, out_ref,
    xin, mall, xw, kf_hi, kf_lo, kb_hi, kb_lo, ext, zland, hland, obuf,
    x_send, x_recv, m_send, m_recv, z_send, z_recv, h_send, h_recv, o_send, o_recv, own_sem,
):
    slices, strip, breadth = init_ref.shape
    angles = meas_ref.shape[1]
    rows = strip * rays
    chunk = breadth // rays
    reach = chunk + 2 * LANE
    me = lax.axis_index("ray")
    cut = lax.axis_index("cuts")
    up, down = lax.rem(cut + 1, cuts), lax.rem(cut + cuts - 1, cuts)
    east, west = lax.rem(me + 1, rays), lax.rem(me + rays - 1, rays)

    barrier = pltpu.get_barrier_semaphore()

    def greet(step, carry):
        peer = lax.rem(me + step, rays)
        pl.semaphore_signal(barrier, inc=1, device_id=(peer, cut), device_id_type=MESH)
        return carry

    lax.fori_loop(1, rays, greet, 0)
    for near in (up, down):
        pl.semaphore_signal(barrier, inc=1, device_id=(me, near), device_id_type=MESH)
    pl.semaphore_wait(barrier, rays + 1)

    def window(place):
        start = jnp.clip(place * chunk - LANE, 0, breadth - reach)
        offset = start - place * chunk + 2 * LANE
        return pl.multiple_of(start, LANE), pl.multiple_of(offset, LANE)

    def x_copy(peer):
        start, offset = window(peer)
        return pltpu.make_async_remote_copy(
            src_ref=init_ref.at[:, :, pl.ds(start, reach)],
            dst_ref=xin.at[me, :, :, pl.ds(offset, reach)],
            send_sem=x_send.at[peer],
            recv_sem=x_recv.at[me],
            device_id=(peer, cut),
            device_id_type=MESH,
        )

    def x_arrival(peer):
        start, offset = window(me)
        return pltpu.make_async_remote_copy(
            src_ref=init_ref.at[:, :, pl.ds(start, reach)],
            dst_ref=xin.at[peer, :, :, pl.ds(offset, reach)],
            send_sem=x_send.at[peer],
            recv_sem=x_recv.at[peer],
            device_id=(peer, cut),
            device_id_type=MESH,
        )

    def m_copy(peer, s):
        start, offset = window(peer)
        return pltpu.make_async_remote_copy(
            src_ref=meas_ref.at[0, :, s, pl.ds(start, reach)],
            dst_ref=mall.at[me, s, :, pl.ds(offset, reach)],
            send_sem=m_send.at[s, peer],
            recv_sem=m_recv.at[s, me],
            device_id=(peer, cut),
            device_id_type=MESH,
        )

    def m_arrival(peer, s):
        start, offset = window(me)
        return pltpu.make_async_remote_copy(
            src_ref=meas_ref.at[0, :, s, pl.ds(start, reach)],
            dst_ref=mall.at[peer, s, :, pl.ds(offset, reach)],
            send_sem=m_send.at[s, peer],
            recv_sem=m_recv.at[s, peer],
            device_id=(peer, cut),
            device_id_type=MESH,
        )

    def each_peer(action):
        def body(step, carry):
            action(lax.rem(me + step, rays))
            return carry

        lax.fori_loop(1, rays, body, 0)

    each_peer(lambda peer: x_copy(peer).start())

    def start_m(peer):
        for s in range(slices):
            m_copy(peer, s).start()

    each_peer(start_m)
    start, offset = window(me)
    own = [
        pltpu.make_async_copy(
            init_ref.at[:, :, pl.ds(start, reach)],
            xin.at[me, :, :, pl.ds(offset, reach)],
            own_sem.at[0],
        )
    ]
    for s in range(slices):
        own.append(
            pltpu.make_async_copy(
                meas_ref.at[0, :, s, pl.ds(start, reach)],
                mall.at[me, s, :, pl.ds(offset, reach)],
                own_sem.at[1 + s],
            )
        )
    for copy in own:
        copy.start()

    def iota(shape, dim):
        return lax.broadcasted_iota(jnp.int32, shape, dim)

    def geometry(subset):
        slot = order_ref[subset]
        picked = angle_ref[pl.ds(slot, 1), :].astype(jnp.float32)
        slope_row = -1.0 + (2.0 * picked + 1.0) / NANG
        wide = jnp.broadcast_to(slope_row, (angles, angles))
        eye = iota((angles, angles), 0) == iota((angles, angles), 1)
        slope_col = jnp.sum(jnp.where(eye, wide, 0.0), axis=1, keepdims=True)
        half = rows // 2
        taps_f = 4
        groups_f = kf_hi.shape[1] // angles
        lane = iota((angles, taps_f * rows), 1)
        position = (lane % rows).astype(jnp.float32) - (rows - 1) / 2.0
        spread = slope_col * position
        tap = lane // rows - half
        for group in range(groups_f):
            place = (tap + taps_f * group).astype(jnp.float32)
            hat = jnp.maximum(1.0 - jnp.abs(place - spread), 0.0)
            high, low = split(hat)
            kf_hi[subset, pl.ds(group * angles, angles), :] = high
            kf_lo[subset, pl.ds(group * angles, angles), :] = low
        taps_b = kb_hi.shape[2] // angles
        groups_b = kb_hi.shape[1] // rows
        slope_wide = jnp.concatenate([slope_row] * taps_b, axis=1)
        lane = iota((rows, taps_b * angles), 1)
        position = iota((rows, taps_b * angles), 0).astype(jnp.float32) - (rows - 1) / 2.0
        spread = slope_wide * position
        tap = lane // angles - half
        for group in range(groups_b):
            place = (tap + taps_b * group).astype(jnp.float32)
            hat = jnp.maximum(1.0 - jnp.abs(place - spread), 0.0)
            high, low = split(hat)
            kb_hi[subset, pl.ds(group * rows, rows), :] = high
            kb_lo[subset, pl.ds(group * rows, rows), :] = low

    for subset in range(SUBSETS):
        geometry(subset)

    own[0].wait()
    each_peer(lambda peer: x_arrival(peer).wait_recv())

    column = iota((rows, reach), 1) + me * chunk - LANE
    inside = (column >= 0) & (column < breadth)
    bin_place = iota((angles, reach), 1) + me * chunk - LANE
    bin_inside = (bin_place >= 0) & (bin_place < breadth)
    for s in range(slices):
        for p in range(rays):
            xw[s, p * strip:(p + 1) * strip, :] = xin[p, s, :, LANE:LANE + reach]
    for s in range(slices):
        xw[s] = jnp.where(inside, xw[s], 0.0)

    ring = chunk + LANE
    half_lane = iota((1, LANE), 1) < LANE // 2

    def circle(value):
        edge = jnp.where(half_lane, value[:, reach - LANE:], value[:, :LANE])
        return jnp.concatenate([value[:, LANE:LANE + chunk], edge], axis=1)

    def turn(value, amount):
        amount = amount % value.shape[1]
        return value if amount == 0 else pltpu.roll(value, amount, 1)

    def project_back(subset, s, slot):
        half = rows // 2
        current = xw[s]
        taps = kf_hi.shape[2] // rows
        stacked = jnp.concatenate([turn(current, j) for j in range(taps)], axis=0)
        lines = dot3(kf_hi[subset], kf_lo[subset], stacked)
        forward = jnp.zeros((angles, reach), jnp.float32)
        for group in range(lines.shape[0] // angles):
            forward += turn(lines[group * angles:(group + 1) * angles], taps * group - half)
        stored = mall[slot, s, :, LANE:LANE + reach]
        residual = circle(jnp.where(bin_inside, stored - forward, 0.0))
        taps = kb_hi.shape[2] // angles
        stacked = jnp.concatenate([turn(residual, -j) for j in range(taps)], axis=0)
        lines = dot3(kb_hi[subset], kb_lo[subset], stacked)
        back = jnp.zeros((rows, ring), jnp.float32)
        for group in range(lines.shape[0] // rows):
            back += turn(lines[group * rows:(group + 1) * rows], half - taps * group)
        return circle(current) + back / (rows * angles)

    ring_lane = iota((rows, ring), 1)
    ring_column = me * chunk + jnp.where(ring_lane < chunk + LANE // 2, ring_lane, ring_lane - ring)
    valid_c = (ring_column >= 0) & (ring_column < breadth - 1)
    valid_r = iota((rows, ring), 0) < rows - 1
    first_slice = cut * slices - 2
    total_slices = slices * cuts

    def tv_pass(source, target, low, high):
        flow_s_before = None
        for t in range(low - 1, high):
            centre = ext[source, t]
            step_s = ext[source, t + 1] - centre
            place = first_slice + t
            step_s = jnp.where((place >= 0) & (place < total_slices - 1), step_s, 0.0)
            step_r = jnp.where(valid_r, pltpu.roll(centre, rows - 1, 0) - centre, 0.0)
            step_c = jnp.where(valid_c, turn(centre, -1) - centre, 0.0)
            inverse = lax.rsqrt(
                step_s * step_s + step_r * step_r + step_c * step_c + TV_EPS * TV_EPS
            )
            flow_s = step_s * inverse
            if t >= low:
                flow_r = step_r * inverse
                flow_c = step_c * inverse
                spread = flow_s - flow_s_before
                spread = spread + flow_r - pltpu.roll(flow_r, 1, 0)
                spread = spread + flow_c - turn(flow_c, 1)
                ext[target, t] = centre + TV_STEP * spread
            flow_s_before = flow_s

    for subset in range(SUBSETS):
        slot = order_ref[subset]
        if subset == 0:
            for copy in own[1:]:
                copy.wait()

            def arrived(peer):
                for s in range(slices):
                    m_arrival(peer, s).wait_recv()

            each_peer(arrived)
        for s in range(slices):
            ext[0, 2 + s] = project_back(subset, s, slot)
        copies = [
            pltpu.make_async_remote_copy(
                src_ref=ext.at[0, pl.ds(2, slices)],
                dst_ref=zland.at[subset, side],
                send_sem=z_send.at[subset, side],
                recv_sem=z_recv.at[subset, side],
                device_id=(me, near),
                device_id_type=MESH,
            )
            for side, near in ((0, up), (1, down))
        ]
        for copy in copies:
            copy.start()
        for copy in copies:
            copy.wait()
        for s in range(slices):
            ext[0, s] = zland[subset, 0, s]
            ext[0, 2 + slices + s] = zland[subset, 1, s]
        tv_pass(0, 1, 1, 3 + slices)
        tv_pass(1, 0, 2, 2 + slices)
        if subset < SUBSETS - 1:
            copies = [
                pltpu.make_async_remote_copy(
                    src_ref=ext.at[0, pl.ds(2, slices), :, pl.ds(lane, LANE)],
                    dst_ref=hland.at[side],
                    send_sem=h_send.at[side],
                    recv_sem=h_recv.at[side],
                    device_id=(near, cut),
                    device_id_type=MESH,
                )
                for side, near, lane in ((0, east, chunk - LANE), (1, west, 0))
            ]
            for copy in copies:
                copy.start()
            for copy in copies:
                copy.wait()
            for s in range(slices):
                joined = jnp.concatenate(
                    [hland[0, s], ext[0, 2 + s, :, :chunk], hland[1, s]], axis=1
                )
                xw[s] = jnp.where(inside, joined, 0.0)

    for s in range(slices):
        for p in range(rays):
            obuf[p, s] = ext[0, 2 + s, p * strip:(p + 1) * strip, :chunk]

    def o_copy(peer):
        return pltpu.make_async_remote_copy(
            src_ref=obuf.at[peer],
            dst_ref=out_ref.at[:, :, pl.ds(pl.multiple_of(me * chunk, LANE), chunk)],
            send_sem=o_send.at[peer],
            recv_sem=o_recv.at[me],
            device_id=(peer, cut),
            device_id_type=MESH,
        )

    def o_arrival(peer):
        return pltpu.make_async_remote_copy(
            src_ref=obuf.at[peer],
            dst_ref=out_ref.at[:, :, pl.ds(pl.multiple_of(peer * chunk, LANE), chunk)],
            send_sem=o_send.at[peer],
            recv_sem=o_recv.at[peer],
            device_id=(peer, cut),
            device_id_type=MESH,
        )

    each_peer(lambda peer: o_copy(peer).start())
    mine = pltpu.make_async_copy(
        obuf.at[me], out_ref.at[:, :, pl.ds(pl.multiple_of(me * chunk, LANE), chunk)], own_sem.at[0]
    )
    mine.start()
    each_peer(lambda peer: o_arrival(peer).wait_recv())
    mine.wait()

    def sent(peer):
        x_copy(peer).wait_send()
        for s in range(slices):
            m_copy(peer, s).wait_send()
        o_copy(peer).wait_send()

    each_peer(sent)


def on_device(rays, cuts, initial, measured, order, angle_index):
    slices, strip, breadth = initial.shape
    angles = measured.shape[1]
    rows = strip * rays
    chunk = breadth // rays
    reach = chunk + 2 * LANE
    ring = chunk + LANE
    taps_f, taps_b = 4, 8
    groups_f = -(-(rows + 1) // taps_f)
    groups_b = -(-(rows + 1) // taps_b)
    dma = pltpu.SemaphoreType.DMA
    f32, bf16 = jnp.float32, jnp.bfloat16
    return pl.pallas_call(
        functools.partial(kernel, rays, cuts),
        out_shape=jax.ShapeDtypeStruct(initial.shape, f32),
        in_specs=[
            pl.BlockSpec(memory_space=pl.ANY),
            pl.BlockSpec(memory_space=pl.ANY),
            pl.BlockSpec(memory_space=pltpu.SMEM),
            pl.BlockSpec(memory_space=pltpu.VMEM),
        ],
        out_specs=pl.BlockSpec(memory_space=pl.ANY),
        scratch_shapes=[
            pltpu.VMEM((rays, slices, strip, reach + 2 * LANE), f32),
            pltpu.VMEM((rays, slices, angles, reach + 2 * LANE), f32),
            pltpu.VMEM((slices, rows, reach), f32),
            pltpu.VMEM((SUBSETS, groups_f * angles, taps_f * rows), bf16),
            pltpu.VMEM((SUBSETS, groups_f * angles, taps_f * rows), bf16),
            pltpu.VMEM((SUBSETS, groups_b * rows, taps_b * angles), bf16),
            pltpu.VMEM((SUBSETS, groups_b * rows, taps_b * angles), bf16),
            pltpu.VMEM((2, slices + 4, rows, ring), f32),
            pltpu.VMEM((SUBSETS, 2, slices, rows, ring), f32),
            pltpu.VMEM((2, slices, rows, LANE), f32),
            pltpu.VMEM((rays, slices, strip, chunk), f32),
            dma((rays,)), dma((rays,)),
            dma((slices, rays)), dma((slices, rays)),
            dma((SUBSETS, 2)), dma((SUBSETS, 2)),
            dma((2,)), dma((2,)),
            dma((rays,)), dma((rays,)),
            dma((1 + slices,)),
        ],
        compiler_params=pltpu.CompilerParams(
            collective_id=0, has_side_effects=True, vmem_limit_bytes=50 * 2**20
        ),
    )(initial, measured, order, angle_index)


def solution(mesh):
    return jax.shard_map(
        functools.partial(on_device, mesh.shape["ray"], mesh.shape["cuts"]),
        mesh=mesh,
        in_specs=(P("cuts", "ray", None), P("ray", None, "cuts", None), P(), P()),
        out_specs=P("cuts", "ray", None),
        check_vma=False,
    )
```

```python
import functools

import jax
import jax.numpy as jnp
from jax import lax
from jax.experimental import pallas as pl
from jax.experimental.pallas import tpu as pltpu
from jax.sharding import PartitionSpec as P

SUBSETS = 2
NANG = 3000
TV_ITERS = 2
TV_STEP = 0.05
TV_EPS = 0.5
MESH = pl.DeviceIdType.MESH
LANE = 128


def split(value):
    high = value.astype(jnp.bfloat16)
    return high, (value - high.astype(jnp.float32)).astype(jnp.bfloat16)


dot = functools.partial(jnp.dot, preferred_element_type=jnp.float32)


def dot2(left, right):
    right_hi, right_lo = split(right)
    return dot(left, right_hi) + dot(left, right_lo)


def dot3(left_hi, left_lo, right):
    right_hi, right_lo = split(right)
    return dot(left_hi, right_hi) + dot(left_lo, right_hi) + dot(left_hi, right_lo)


def band_rows(rows, taps):
    half = rows // 2
    kept = []
    for group in range(-(-(rows + 1) // taps)):
        first = taps * group - half
        nearest = min(abs(first + j) for j in range(taps))
        ends = sum(1 for i in range(half) if half - 0.5 - i > nearest - 1)
        kept.append(min(half, -(-ends // 8) * 8))
    return kept


FAR_FIRST = (10, 11, 14, 15, 6, 7, 8, 9, 2, 3, 12, 13, 4, 5, 1)


def partner(me, mask):
    return sum(
        bit * (1 - (me // bit) % 2 if mask & bit else (me // bit) % 2) for bit in (1, 2, 4, 8)
    )


def chunk_of(ray):
    core, high, y = ray % 2, (ray // 2) % 2, ray // 4
    return 2 * (y + high * (7 - 2 * y)) + core


def ray_of(chunk):
    core, spot = chunk % 2, chunk // 2
    high = spot // 4
    y = spot + high * (7 - 2 * spot)
    return (y * 2 + high) * 2 + core


def kernel(
    rays, cuts,
    init_ref, meas_ref, order_in, angle_in, out_ref,
    order_ref, angle_ref, mv, xin, m_mid, m_all, m_edge, xw, kf, kb_hi, kb_lo,
    ext, pack, zland, pland, hland, obuf,
    x_send, x_recv, a_send, a_recv, z_send, z_recv, p_send, p_recv,
    h_send, h_recv, e_send, e_recv, o_send, o_recv, own_sem,
):
    slices, strip, breadth = init_ref.shape
    angles = meas_ref.shape[1]
    rows = strip * rays
    chunk = breadth // rays
    reach = chunk + 2 * LANE
    ring = chunk + LANE
    me = lax.axis_index("ray")
    cut = lax.axis_index("cuts")
    place = chunk_of(me)
    up, down = lax.rem(cut + 1, cuts), lax.rem(cut + cuts - 1, cuts)
    east, west = ray_of(lax.rem(place + 1, rays)), ray_of(lax.rem(place + rays - 1, rays))
    peers = [partner(me, mask) for mask in FAR_FIRST]

    barrier = pltpu.get_barrier_semaphore()
    for peer in peers:
        pl.semaphore_signal(barrier, inc=1, device_id=(peer, cut), device_id_type=MESH)
    for near in (up, down):
        pl.semaphore_signal(barrier, inc=1, device_id=(me, near), device_id_type=MESH)

    def window(spot):
        start = jnp.clip(spot * chunk - LANE, 0, breadth - reach)
        offset = start - spot * chunk + 2 * LANE
        return pl.multiple_of(start, LANE), pl.multiple_of(offset, LANE)

    local = [
        pltpu.make_async_copy(order_in, order_ref, own_sem.at[0]),
        pltpu.make_async_copy(angle_in, angle_ref, own_sem.at[1]),
    ]
    start, offset = window(place)
    mine = pltpu.make_async_copy(
        init_ref.at[:, :, pl.ds(start, reach)],
        xin.at[me, :, :, pl.ds(offset, reach)],
        own_sem.at[2],
    )
    held = [
        pltpu.make_async_copy(meas_ref.at[0, :, s], mv.at[s], own_sem.at[3 + s])
        for s in range(slices)
    ]
    for copy in [*local, *held, mine]:
        copy.start()

    def send(src, dst, send_sem, recv_sem, target):
        return pltpu.make_async_remote_copy(
            src_ref=src, dst_ref=dst, send_sem=send_sem, recv_sem=recv_sem,
            device_id=target, device_id_type=MESH,
        )

    def x_copy(peer, arriving):
        start, offset = window(place if arriving else chunk_of(peer))
        origin = peer if arriving else me
        return send(
            init_ref.at[:, :, pl.ds(start, reach)],
            xin.at[origin, :, :, pl.ds(offset, reach)],
            x_send.at[peer], x_recv.at[origin], (peer, cut),
        )

    def a_copy(peer, arriving):
        column = pl.multiple_of(chunk * (place if arriving else chunk_of(peer)), chunk)
        origin = peer if arriving else me
        return send(
            mv.at[:, :, pl.ds(column, chunk)], m_all.at[origin],
            a_send.at[peer], a_recv.at[origin], (peer, cut),
        )

    def o_copy(peer, arriving):
        column = pl.multiple_of(chunk * (chunk_of(peer) if arriving else place), chunk)
        origin = peer if arriving else me
        return send(
            obuf.at[peer], out_ref.at[:, :, pl.ds(column, chunk)],
            o_send.at[peer], o_recv.at[origin], (peer, cut),
        )

    def iota(shape, dim):
        return lax.broadcasted_iota(jnp.int32, shape, dim)

    half = rows // 2
    taps_f = kf.shape[2] // rows
    taps_b = kb_hi.shape[2] // angles
    bands = band_rows(rows, taps_b)

    def geometry(subset):
        slot = order_ref[subset]
        picked = angle_ref[pl.ds(slot, 1), :].astype(jnp.float32)
        slope_row = -1.0 + (2.0 * picked + 1.0) / NANG
        wide = jnp.broadcast_to(slope_row, (angles, angles))
        eye = iota((angles, angles), 0) == iota((angles, angles), 1)
        slope_col = jnp.sum(jnp.where(eye, wide, 0.0), axis=1, keepdims=True)
        lane = iota((angles, taps_f * rows), 1)
        position = (lane % rows).astype(jnp.float32) - (rows - 1) / 2.0
        spread = jnp.floor(slope_col * position * 256.0 + 0.5) / 256.0
        tap = lane // rows - half
        for group in range(kf.shape[1] // angles):
            reached = (tap + taps_f * group).astype(jnp.float32)
            hat = jnp.maximum(1.0 - jnp.abs(reached - spread), 0.0)
            kf[subset, group * angles:(group + 1) * angles, :] = hat.astype(jnp.bfloat16)
        slope_wide = jnp.concatenate([slope_row] * taps_b, axis=1)
        lane = iota((rows, taps_b * angles), 1)
        position = iota((rows, taps_b * angles), 0).astype(jnp.float32) - (rows - 1) / 2.0
        spread = slope_wide * position
        tap = lane // angles - half
        line = 0
        for group, ends in enumerate(bands):
            reached = (tap + taps_b * group).astype(jnp.float32)
            hat = jnp.maximum(1.0 - jnp.abs(reached - spread), 0.0)
            if 2 * ends < rows:
                hat = jnp.concatenate([hat[:ends], hat[rows - ends:]], axis=0)
            high, low = split(hat)
            kb_hi[subset, line:line + 2 * ends, :] = high
            kb_lo[subset, line:line + 2 * ends, :] = low
            line += 2 * ends

    for copy in local:
        copy.wait()
    for subset in range(SUBSETS):
        geometry(subset)
    pl.semaphore_wait(barrier, rays + 1)

    for peer in peers:
        x_copy(peer, False).start()
    for copy in held:
        copy.wait()

    for peer in peers:
        a_copy(peer, False).start()
    column = pl.multiple_of(chunk * place, chunk)
    m_all[me] = mv[:, :, pl.ds(column, chunk)]

    start, offset = window(place)
    mine.wait()
    for peer in peers:
        x_copy(peer, True).wait_recv()

    column = iota((1, reach), 1) + place * chunk - LANE
    inside = (column >= 0) & (column < breadth)
    for s in range(slices):
        for p in range(rays):
            part = xin[p, s, :, LANE:LANE + reach]
            xw[s, p * strip:(p + 1) * strip, :] = jnp.where(inside, part, 0.0)

    half_lane = iota((1, LANE), 1) < LANE // 2

    def circle(value):
        edge = jnp.where(half_lane, value[:, reach - LANE:], value[:, :LANE])
        return jnp.concatenate([value[:, LANE:LANE + chunk], edge], axis=1)

    def turn(value, amount):
        amount = amount % value.shape[1]
        return value if amount == 0 else pltpu.roll(value, amount, 1)

    def project(subset, s):
        current = xw[s]
        stacked = jnp.concatenate([turn(current, j) for j in range(taps_f)], axis=0)
        lines = dot2(kf[subset], stacked)
        forward = jnp.zeros((angles, reach), jnp.float32)
        for group in range(kf.shape[1] // angles):
            forward += turn(lines[group * angles:(group + 1) * angles], taps_f * group - half)
        return forward

    def back_project(subset, s, forward, stored):
        residual = circle(jnp.where(inside, stored - forward, 0.0))
        stacked = jnp.concatenate([turn(residual, -j) for j in range(taps_b)], axis=0)
        lines = dot3(kb_hi[subset], kb_lo[subset], stacked)
        blocks = [jnp.zeros((8, ring), jnp.float32) for _ in range(rows // 8)]
        line = 0
        for group, ends in enumerate(bands):
            turned = turn(lines[line:line + 2 * ends], half - taps_b * group)
            line += 2 * ends
            for at in range(2 * ends // 8):
                row = at if at < ends // 8 else at + (rows - 2 * ends) // 8
                blocks[row] = blocks[row] + turned[at * 8:(at + 1) * 8]
        return circle(xw[s]) + jnp.concatenate(blocks, axis=0) / (rows * angles)

    lane = iota((1, ring), 1)
    ring_column = place * chunk + jnp.where(lane < chunk + LANE // 2, lane, lane - ring)
    valid_c = (ring_column >= 0) & (ring_column < breadth - 1)
    valid_r = iota((rows, 1), 0) < rows - 1
    first_slice = cut * slices - 2
    total_slices = slices * cuts

    def tv_pass(source, target, low, high):
        before = None
        for t in range(low - 1, high):
            centre = ext[source, t]
            step_s = ext[source, t + 1] - centre
            at = first_slice + t
            step_s = jnp.where((at >= 0) & (at < total_slices - 1), step_s, 0.0)
            step_r = jnp.where(valid_r, pltpu.roll(centre, rows - 1, 0) - centre, 0.0)
            step_c = jnp.where(valid_c, turn(centre, -1) - centre, 0.0)
            inverse = lax.rsqrt(
                step_s * step_s + step_r * step_r + step_c * step_c + TV_EPS * TV_EPS
            )
            flow_s = step_s * inverse
            if t >= low:
                flow_r = step_r * inverse
                flow_c = step_c * inverse
                spread = flow_s - before
                spread = spread + flow_r - pltpu.roll(flow_r, 1, 0)
                spread = spread + flow_c - turn(flow_c, 1)
                ext[target, t] = centre + TV_STEP * spread
            before = flow_s

    def gather_measured():
        for peer in peers:
            a_copy(peer, True).wait_recv()
        copies = []
        for subset in range(SUBSETS):
            m_mid[subset] = m_all[order_ref[subset]]
            copies.append([
                send(
                    m_mid.at[subset, :, :, pl.ds(at, LANE)], m_edge.at[subset, side],
                    e_send.at[subset, side], e_recv.at[subset, side], (near, cut),
                )
                for side, near, at in ((0, east, chunk - LANE), (1, west, 0))
            ])
            for copy in copies[-1]:
                copy.start()
        return copies

    octets = rows // 8
    pack_lane = iota((1, LANE), 1) // 4

    for subset in range(SUBSETS):
        for s in range(slices):
            forward = project(subset, s)
            if s == 0 and subset == 0:
                edge_copies = gather_measured()
            if s == 0:
                for copy in edge_copies[subset]:
                    copy.wait_recv()
            stored = jnp.concatenate(
                [m_edge[subset, 0, s], m_mid[subset, s], m_edge[subset, 1, s]], axis=1
            )
            ext[0, 2 + s] = back_project(subset, s, forward, stored)
            for side, near in ((0, up), (1, down)):
                send(
                    ext.at[0, 2 + s, :, pl.ds(0, chunk)], zland.at[subset, side, s],
                    z_send.at[subset, side, s], z_recv.at[subset, side, s], (me, near),
                ).start()
        packed = jnp.zeros((8, LANE), jnp.float32)
        for s in range(slices):
            for g in range(octets):
                k = octets * s + g
                edge = ext[0, 2 + s, g * 8:(g + 1) * 8, chunk:]
                packed = jnp.where(pack_lane == k, turn(edge, 2 + 4 * k), packed)
        pack[subset] = packed
        for side, near in ((0, up), (1, down)):
            send(
                pack.at[subset], pland.at[subset, side],
                p_send.at[subset, side], p_recv.at[subset, side], (me, near),
            ).start()
        for side, near in ((0, up), (1, down)):
            for s in range(slices):
                send(
                    ext.at[0, 2 + s, :, pl.ds(0, chunk)], zland.at[subset, side, s],
                    z_send.at[subset, side, s], z_recv.at[subset, side, s], (me, near),
                ).wait()
            send(
                pack.at[subset], pland.at[subset, side],
                p_send.at[subset, side], p_recv.at[subset, side], (me, near),
            ).wait()
            base = (2 + slices) * side
            packed = pland[subset, side]
            for s in range(slices):
                ext[0, base + s, :, :chunk] = zland[subset, side, s]
                for g in range(octets):
                    k = octets * s + g
                    ext[0, base + s, g * 8:(g + 1) * 8, chunk:] = turn(packed, -(2 + 4 * k))
        tv_pass(0, 1, 1, 3 + slices)
        tv_pass(1, 0, 2, 2 + slices)
        if subset < SUBSETS - 1:
            side_copies = [
                send(
                    ext.at[0, pl.ds(2, slices), :, pl.ds(at, LANE)], hland.at[side],
                    h_send.at[side], h_recv.at[side], (near, cut),
                )
                for side, near, at in ((0, east, chunk - LANE), (1, west, 0))
            ]
            for copy in side_copies:
                copy.start()
            for copy in side_copies:
                copy.wait()
            for s in range(slices):
                joined = jnp.concatenate(
                    [hland[0, s], ext[0, 2 + s, :, :chunk], hland[1, s]], axis=1
                )
                xw[s] = jnp.where(inside, joined, 0.0)

    for s in range(slices):
        for p in range(rays):
            obuf[p, s] = ext[0, 2 + s, p * strip:(p + 1) * strip, :chunk]
    for peer in peers:
        o_copy(peer, False).start()
    column = pl.multiple_of(place * chunk, chunk)
    last = pltpu.make_async_copy(obuf.at[me], out_ref.at[:, :, pl.ds(column, chunk)], own_sem.at[2])
    last.start()

    for peer in peers:
        x_copy(peer, False).wait_send()
        a_copy(peer, False).wait_send()
    for copies in edge_copies:
        for copy in copies:
            copy.wait_send()

    for peer in peers:
        o_copy(peer, True).wait_recv()
    for peer in peers:
        o_copy(peer, False).wait_send()
    last.wait()


def on_device(rays, cuts, initial, measured, order, angle_index):
    slices, strip, breadth = initial.shape
    angles = measured.shape[1]
    rows = strip * rays
    chunk = breadth // rays
    reach = chunk + 2 * LANE
    ring = chunk + LANE
    taps_f, taps_b = 4, 8
    groups_f = -(-(rows + 1) // taps_f)
    lines_b = 2 * sum(band_rows(rows, taps_b))
    dma = pltpu.SemaphoreType.DMA
    f32, bf16 = jnp.float32, jnp.bfloat16
    anywhere = pl.BlockSpec(memory_space=pl.ANY)

    return pl.pallas_call(
        functools.partial(kernel, rays, cuts),
        out_shape=jax.ShapeDtypeStruct(initial.shape, f32),
        in_specs=[anywhere] * 4,
        out_specs=anywhere,
        scratch_shapes=[
            pltpu.SMEM(order.shape, jnp.int32),
            pltpu.VMEM(angle_index.shape, jnp.int32),
            pltpu.VMEM((slices, angles, breadth), f32),
            pltpu.VMEM((rays, slices, strip, reach + 2 * LANE), f32),
            pltpu.VMEM((SUBSETS, slices, angles, chunk), f32),
            pltpu.VMEM((rays, slices, angles, chunk), f32),
            pltpu.VMEM((SUBSETS, 2, slices, angles, LANE), f32),
            pltpu.VMEM((slices, rows, reach), f32),
            pltpu.VMEM((SUBSETS, groups_f * angles, taps_f * rows), bf16),
            pltpu.VMEM((SUBSETS, lines_b, taps_b * angles), bf16),
            pltpu.VMEM((SUBSETS, lines_b, taps_b * angles), bf16),
            pltpu.VMEM((2, slices + 4, rows, ring), f32),
            pltpu.VMEM((SUBSETS, 8, LANE), f32),
            pltpu.VMEM((SUBSETS, 2, slices, rows, chunk), f32),
            pltpu.VMEM((SUBSETS, 2, 8, LANE), f32),
            pltpu.VMEM((2, slices, rows, LANE), f32),
            pltpu.VMEM((rays, slices, strip, chunk), f32),
            dma((rays,)), dma((rays,)),
            dma((rays,)), dma((rays,)),
            dma((SUBSETS, 2, slices)), dma((SUBSETS, 2, slices)),
            dma((SUBSETS, 2)), dma((SUBSETS, 2)),
            dma((2,)), dma((2,)),
            dma((SUBSETS, 2)), dma((SUBSETS, 2)),
            dma((rays,)), dma((rays,)),
            dma((3 + slices,)),
        ],
        compiler_params=pltpu.CompilerParams(
            collective_id=0, has_side_effects=True, vmem_limit_bytes=60 * 2**20
        ),
    )(initial, measured, order, angle_index)


def solution(mesh):
    return jax.shard_map(
        functools.partial(on_device, mesh.shape["ray"], mesh.shape["cuts"]),
        mesh=mesh,
        in_specs=(P("cuts", "ray", None), P("ray", None, "cuts", None), P(), P()),
        out_specs=P("cuts", "ray", None),
        check_vma=False,
    )
```

```python
import functools

import jax
import jax.numpy as jnp
from jax import lax
from jax.experimental import pallas as pl
from jax.experimental.pallas import tpu as pltpu
from jax.sharding import PartitionSpec as P

SUBSETS = 2
NANG = 3000
TV_ITERS = 2
TV_STEP = 0.05
TV_EPS = 0.5
MESH = pl.DeviceIdType.MESH
LANE = 128


def split(value):
    high = value.astype(jnp.bfloat16)
    return high, (value - high.astype(jnp.float32)).astype(jnp.bfloat16)


dot = functools.partial(jnp.dot, preferred_element_type=jnp.float32)


def dot2(left, right):
    right_hi, right_lo = split(right)
    return dot(left, right_hi) + dot(left, right_lo)


def dot3(left_hi, left_lo, right):
    right_hi, right_lo = split(right)
    return dot(left_hi, right_hi) + dot(left_lo, right_hi) + dot(left_hi, right_lo)


def band_rows(rows, taps):
    half = rows // 2
    kept = []
    for group in range(-(-(rows + 1) // taps)):
        first = taps * group - half
        nearest = min(abs(first + j) for j in range(taps))
        ends = sum(1 for i in range(half) if half - 0.5 - i > nearest - 1)
        kept.append(min(half, -(-ends // 8) * 8))
    return kept


FAR_FIRST = (10, 11, 14, 15, 6, 7, 8, 9, 2, 3, 12, 13, 4, 5, 1)


def partner(me, mask):
    return sum(
        bit * (1 - (me // bit) % 2 if mask & bit else (me // bit) % 2) for bit in (1, 2, 4, 8)
    )


def chunk_of(ray):
    core, high, y = ray % 2, (ray // 2) % 2, ray // 4
    return 2 * (y + high * (7 - 2 * y)) + core


def ray_of(chunk):
    core, spot = chunk % 2, chunk // 2
    high = spot // 4
    y = spot + high * (7 - 2 * spot)
    return (y * 2 + high) * 2 + core


def kernel(
    rays, cuts,
    init_ref, meas_ref, order_in, angle_in, out_ref,
    order_ref, angle_ref, mv, m_mate, m_pick, xin, m_mid, m_all0, m_all1, m_edge, xw, kf, kb_hi, kb_lo,
    ext, pack, zland, pland, hland, obuf,
    x_send, x_recv, t_send, t_recv, a_send, a_recv, z_send, z_recv, p_send, p_recv,
    h_send, h_recv, e_send, e_recv, o_send, o_recv, own_sem,
):
    slices, strip, breadth = init_ref.shape
    angles = meas_ref.shape[1]
    rows = strip * rays
    chunk = breadth // rays
    reach = chunk + 2 * LANE
    ring = chunk + LANE
    me = lax.axis_index("ray")
    cut = lax.axis_index("cuts")
    place = chunk_of(me)
    up, down = lax.rem(cut + 1, cuts), lax.rem(cut + cuts - 1, cuts)
    east, west = ray_of(lax.rem(place + 1, rays)), ray_of(lax.rem(place + rays - 1, rays))
    peers = [partner(me, mask) for mask in FAR_FIRST]
    core, mate = me % 2, partner(me, 1)
    alike = [partner(me, mask) for mask in FAR_FIRST if mask % 2 == 0]
    m_all = (m_all0, m_all1)
    pairs = rays // 2

    barrier = pltpu.get_barrier_semaphore()
    for peer in peers:
        pl.semaphore_signal(barrier, inc=1, device_id=(peer, cut), device_id_type=MESH)
    for near in (up, down):
        pl.semaphore_signal(barrier, inc=1, device_id=(me, near), device_id_type=MESH)

    def window(spot):
        start = jnp.clip(spot * chunk - LANE, 0, breadth - reach)
        offset = start - spot * chunk + 2 * LANE
        return pl.multiple_of(start, LANE), pl.multiple_of(offset, LANE)

    local = [
        pltpu.make_async_copy(order_in, order_ref, own_sem.at[0]),
        pltpu.make_async_copy(angle_in, angle_ref, own_sem.at[1]),
    ]
    start, offset = window(place)
    mine = pltpu.make_async_copy(
        init_ref.at[:, :, pl.ds(start, reach)],
        xin.at[me, :, :, pl.ds(offset, reach)],
        own_sem.at[2],
    )
    held = [
        pltpu.make_async_copy(meas_ref.at[0, :, s], mv.at[s], own_sem.at[3 + s])
        for s in range(slices)
    ]
    for copy in [*local, *held, mine]:
        copy.start()

    def send(src, dst, send_sem, recv_sem, target):
        return pltpu.make_async_remote_copy(
            src_ref=src, dst_ref=dst, send_sem=send_sem, recv_sem=recv_sem,
            device_id=target, device_id_type=MESH,
        )

    def x_copy(peer, arriving):
        start, offset = window(place if arriving else chunk_of(peer))
        origin = peer if arriving else me
        return send(
            init_ref.at[:, :, pl.ds(start, reach)],
            xin.at[origin, :, :, pl.ds(offset, reach)],
            x_send.at[peer], x_recv.at[origin], (peer, cut),
        )

    def mate_copy(pair):
        theirs = pl.multiple_of(chunk * (2 * pair + 1 - core), chunk)
        return send(
            mv.at[:, :, pl.ds(theirs, chunk)], m_mate.at[pair],
            t_send.at[pair], t_recv.at[pair], (mate, cut),
        )

    def a_copy(subset, peer, arriving):
        origin = peer if arriving else me
        return send(
            m_pick.at[subset, (place if arriving else chunk_of(peer)) // 2],
            m_all[subset].at[origin // 2],
            a_send.at[subset, peer // 2], a_recv.at[subset, origin // 2], (peer, cut),
        )

    def o_copy(peer, arriving):
        column = pl.multiple_of(chunk * (chunk_of(peer) if arriving else place), chunk)
        origin = peer if arriving else me
        return send(
            obuf.at[peer], out_ref.at[:, :, pl.ds(column, chunk)],
            o_send.at[peer], o_recv.at[origin], (peer, cut),
        )

    def iota(shape, dim):
        return lax.broadcasted_iota(jnp.int32, shape, dim)

    half = rows // 2
    taps_f = kf.shape[2] // rows
    taps_b = kb_hi.shape[2] // angles
    bands = band_rows(rows, taps_b)

    def geometry(subset):
        slot = order_ref[subset]
        picked = angle_ref[pl.ds(slot, 1), :].astype(jnp.float32)
        slope_row = -1.0 + (2.0 * picked + 1.0) / NANG
        wide = jnp.broadcast_to(slope_row, (angles, angles))
        eye = iota((angles, angles), 0) == iota((angles, angles), 1)
        slope_col = jnp.sum(jnp.where(eye, wide, 0.0), axis=1, keepdims=True)
        lane = iota((angles, taps_f * rows), 1)
        position = (lane % rows).astype(jnp.float32) - (rows - 1) / 2.0
        spread = jnp.floor(slope_col * position * 256.0 + 0.5) / 256.0
        tap = lane // rows - half
        for group in range(kf.shape[1] // angles):
            reached = (tap + taps_f * group).astype(jnp.float32)
            hat = jnp.maximum(1.0 - jnp.abs(reached - spread), 0.0)
            kf[subset, group * angles:(group + 1) * angles, :] = hat.astype(jnp.bfloat16)
        slope_wide = jnp.concatenate([slope_row] * taps_b, axis=1)
        lane = iota((rows, taps_b * angles), 1)
        position = iota((rows, taps_b * angles), 0).astype(jnp.float32) - (rows - 1) / 2.0
        spread = slope_wide * position
        tap = lane // angles - half
        line = 0
        for group, ends in enumerate(bands):
            reached = (tap + taps_b * group).astype(jnp.float32)
            hat = jnp.maximum(1.0 - jnp.abs(reached - spread), 0.0)
            if 2 * ends < rows:
                hat = jnp.concatenate([hat[:ends], hat[rows - ends:]], axis=0)
            high, low = split(hat)
            kb_hi[subset, line:line + 2 * ends, :] = high
            kb_lo[subset, line:line + 2 * ends, :] = low
            line += 2 * ends

    for copy in local:
        copy.wait()
    for subset in range(SUBSETS):
        geometry(subset)
    pl.semaphore_wait(barrier, rays + 1)

    for copy in held:
        copy.wait()
    for pair in range(pairs):
        mate_copy(pair).start()
    for peer in peers:
        x_copy(peer, False).start()
    for pair in range(pairs):
        mate_copy(pair).wait_recv()
    def hand_on(subset):
        ours = order_ref[subset] == me
        for pair in range(pairs):
            column = pl.multiple_of(chunk * (2 * pair + core), chunk)
            m_pick[subset, pair] = jnp.where(ours, mv[:, :, pl.ds(column, chunk)], m_mate[pair])
        for peer in alike:
            a_copy(subset, peer, False).start()
        m_all[subset][me // 2] = m_pick[subset, place // 2]

    hand_on(0)

    start, offset = window(place)
    mine.wait()
    for peer in peers:
        x_copy(peer, True).wait_recv()

    column = iota((1, reach), 1) + place * chunk - LANE
    inside = (column >= 0) & (column < breadth)
    for s in range(slices):
        for p in range(rays):
            part = xin[p, s, :, LANE:LANE + reach]
            xw[s, p * strip:(p + 1) * strip, :] = jnp.where(inside, part, 0.0)

    half_lane = iota((1, LANE), 1) < LANE // 2

    def circle(value):
        edge = jnp.where(half_lane, value[:, reach - LANE:], value[:, :LANE])
        return jnp.concatenate([value[:, LANE:LANE + chunk], edge], axis=1)

    def turn(value, amount):
        amount = amount % value.shape[1]
        return value if amount == 0 else pltpu.roll(value, amount, 1)

    def project(subset, s):
        current = xw[s]
        stacked = jnp.concatenate([turn(current, j) for j in range(taps_f)], axis=0)
        lines = dot2(kf[subset], stacked)
        forward = jnp.zeros((angles, reach), jnp.float32)
        for group in range(kf.shape[1] // angles):
            forward += turn(lines[group * angles:(group + 1) * angles], taps_f * group - half)
        return forward

    def back_project(subset, s, forward, stored):
        residual = circle(jnp.where(inside, stored - forward, 0.0))
        stacked = jnp.concatenate([turn(residual, -j) for j in range(taps_b)], axis=0)
        lines = dot3(kb_hi[subset], kb_lo[subset], stacked)
        blocks = [jnp.zeros((8, ring), jnp.float32) for _ in range(rows // 8)]
        line = 0
        for group, ends in enumerate(bands):
            turned = turn(lines[line:line + 2 * ends], half - taps_b * group)
            line += 2 * ends
            for at in range(2 * ends // 8):
                row = at if at < ends // 8 else at + (rows - 2 * ends) // 8
                blocks[row] = blocks[row] + turned[at * 8:(at + 1) * 8]
        return circle(xw[s]) + jnp.concatenate(blocks, axis=0) / (rows * angles)

    lane = iota((1, ring), 1)
    ring_column = place * chunk + jnp.where(lane < chunk + LANE // 2, lane, lane - ring)
    valid_c = (ring_column >= 0) & (ring_column < breadth - 1)
    valid_r = iota((rows, 1), 0) < rows - 1
    first_slice = cut * slices - 2
    total_slices = slices * cuts

    def tv_pass(source, target, low, high):
        before = None
        for t in range(low - 1, high):
            centre = ext[source, t]
            step_s = ext[source, t + 1] - centre
            at = first_slice + t
            step_s = jnp.where((at >= 0) & (at < total_slices - 1), step_s, 0.0)
            step_r = jnp.where(valid_r, pltpu.roll(centre, rows - 1, 0) - centre, 0.0)
            step_c = jnp.where(valid_c, turn(centre, -1) - centre, 0.0)
            inverse = lax.rsqrt(
                step_s * step_s + step_r * step_r + step_c * step_c + TV_EPS * TV_EPS
            )
            flow_s = step_s * inverse
            if t >= low:
                flow_r = step_r * inverse
                flow_c = step_c * inverse
                spread = flow_s - before
                spread = spread + flow_r - pltpu.roll(flow_r, 1, 0)
                spread = spread + flow_c - turn(flow_c, 1)
                ext[target, t] = centre + TV_STEP * spread
            before = flow_s

    def gather_measured(subset):
        for peer in alike:
            a_copy(subset, peer, True).wait_recv()
        m_mid[subset] = m_all[subset][order_ref[subset] // 2]
        copies = [
            send(
                m_mid.at[subset, :, :, pl.ds(at, LANE)], m_edge.at[subset, side],
                e_send.at[subset, side], e_recv.at[subset, side], (near, cut),
            )
            for side, near, at in ((0, east, chunk - LANE), (1, west, 0))
        ]
        for copy in copies:
            copy.start()
        return copies

    octets = rows // 8
    pack_lane = iota((1, LANE), 1) // 4

    for subset in range(SUBSETS):
        for s in range(slices):
            forward = project(subset, s)
            if s == 0 and subset == 0:
                edge_copies = [gather_measured(subset)]
                hand_on(1)
            if s == 0:
                for copy in edge_copies[subset]:
                    copy.wait_recv()
            stored = jnp.concatenate(
                [m_edge[subset, 0, s], m_mid[subset, s], m_edge[subset, 1, s]], axis=1
            )
            ext[0, 2 + s] = back_project(subset, s, forward, stored)
            for side, near in ((0, up), (1, down)):
                send(
                    ext.at[0, 2 + s, :, pl.ds(0, chunk)], zland.at[subset, side, s],
                    z_send.at[subset, side, s], z_recv.at[subset, side, s], (me, near),
                ).start()
        packed = jnp.zeros((8, LANE), jnp.float32)
        for s in range(slices):
            for g in range(octets):
                k = octets * s + g
                edge = ext[0, 2 + s, g * 8:(g + 1) * 8, chunk:]
                packed = jnp.where(pack_lane == k, turn(edge, 2 + 4 * k), packed)
        pack[subset] = packed
        for side, near in ((0, up), (1, down)):
            send(
                pack.at[subset], pland.at[subset, side],
                p_send.at[subset, side], p_recv.at[subset, side], (me, near),
            ).start()
        for side, near in ((0, up), (1, down)):
            for s in range(slices):
                send(
                    ext.at[0, 2 + s, :, pl.ds(0, chunk)], zland.at[subset, side, s],
                    z_send.at[subset, side, s], z_recv.at[subset, side, s], (me, near),
                ).wait()
            send(
                pack.at[subset], pland.at[subset, side],
                p_send.at[subset, side], p_recv.at[subset, side], (me, near),
            ).wait()
            base = (2 + slices) * side
            packed = pland[subset, side]
            for s in range(slices):
                ext[0, base + s, :, :chunk] = zland[subset, side, s]
                for g in range(octets):
                    k = octets * s + g
                    ext[0, base + s, g * 8:(g + 1) * 8, chunk:] = turn(packed, -(2 + 4 * k))
        tv_pass(0, 1, 1, 3 + slices)
        tv_pass(1, 0, 2, 2 + slices)
        if subset < SUBSETS - 1:
            side_copies = [
                send(
                    ext.at[0, pl.ds(2, slices), :, pl.ds(at, LANE)], hland.at[side],
                    h_send.at[side], h_recv.at[side], (near, cut),
                )
                for side, near, at in ((0, east, chunk - LANE), (1, west, 0))
            ]
            for copy in side_copies:
                copy.start()
            edge_copies.append(gather_measured(subset + 1))
            for copy in side_copies:
                copy.wait()
            for s in range(slices):
                joined = jnp.concatenate(
                    [hland[0, s], ext[0, 2 + s, :, :chunk], hland[1, s]], axis=1
                )
                xw[s] = jnp.where(inside, joined, 0.0)

    for s in range(slices):
        for p in range(rays):
            obuf[p, s] = ext[0, 2 + s, p * strip:(p + 1) * strip, :chunk]
    for peer in peers:
        o_copy(peer, False).start()
    column = pl.multiple_of(place * chunk, chunk)
    last = pltpu.make_async_copy(obuf.at[me], out_ref.at[:, :, pl.ds(column, chunk)], own_sem.at[2])
    last.start()

    for peer in peers:
        x_copy(peer, False).wait_send()
    for pair in range(pairs):
        mate_copy(pair).wait_send()
    for subset in range(SUBSETS):
        for peer in alike:
            a_copy(subset, peer, False).wait_send()
    for copies in edge_copies:
        for copy in copies:
            copy.wait_send()

    for peer in peers:
        o_copy(peer, True).wait_recv()
    for peer in peers:
        o_copy(peer, False).wait_send()
    last.wait()


def on_device(rays, cuts, initial, measured, order, angle_index):
    slices, strip, breadth = initial.shape
    angles = measured.shape[1]
    rows = strip * rays
    chunk = breadth // rays
    reach = chunk + 2 * LANE
    ring = chunk + LANE
    taps_f, taps_b = 4, 8
    groups_f = -(-(rows + 1) // taps_f)
    lines_b = 2 * sum(band_rows(rows, taps_b))
    dma = pltpu.SemaphoreType.DMA
    f32, bf16 = jnp.float32, jnp.bfloat16
    anywhere = pl.BlockSpec(memory_space=pl.ANY)

    return pl.pallas_call(
        functools.partial(kernel, rays, cuts),
        out_shape=jax.ShapeDtypeStruct(initial.shape, f32),
        in_specs=[anywhere] * 4,
        out_specs=anywhere,
        scratch_shapes=[
            pltpu.SMEM(order.shape, jnp.int32),
            pltpu.VMEM(angle_index.shape, jnp.int32),
            pltpu.VMEM((slices, angles, breadth), f32),
            pltpu.VMEM((rays // 2, slices, angles, chunk), f32),
            pltpu.VMEM((SUBSETS, rays // 2, slices, angles, chunk), f32),
            pltpu.VMEM((rays, slices, strip, reach + 2 * LANE), f32),
            pltpu.VMEM((SUBSETS, slices, angles, chunk), f32),
            pltpu.VMEM((rays // 2, slices, angles, chunk), f32),
            pltpu.VMEM((rays // 2, slices, angles, chunk), f32),
            pltpu.VMEM((SUBSETS, 2, slices, angles, LANE), f32),
            pltpu.VMEM((slices, rows, reach), f32),
            pltpu.VMEM((SUBSETS, groups_f * angles, taps_f * rows), bf16),
            pltpu.VMEM((SUBSETS, lines_b, taps_b * angles), bf16),
            pltpu.VMEM((SUBSETS, lines_b, taps_b * angles), bf16),
            pltpu.VMEM((2, slices + 4, rows, ring), f32),
            pltpu.VMEM((SUBSETS, 8, LANE), f32),
            pltpu.VMEM((SUBSETS, 2, slices, rows, chunk), f32),
            pltpu.VMEM((SUBSETS, 2, 8, LANE), f32),
            pltpu.VMEM((2, slices, rows, LANE), f32),
            pltpu.VMEM((rays, slices, strip, chunk), f32),
            dma((rays,)), dma((rays,)),
            dma((rays // 2,)), dma((rays // 2,)),
            dma((SUBSETS, rays // 2)), dma((SUBSETS, rays // 2)),
            dma((SUBSETS, 2, slices)), dma((SUBSETS, 2, slices)),
            dma((SUBSETS, 2)), dma((SUBSETS, 2)),
            dma((2,)), dma((2,)),
            dma((SUBSETS, 2)), dma((SUBSETS, 2)),
            dma((rays,)), dma((rays,)),
            dma((3 + slices,)),
        ],
        compiler_params=pltpu.CompilerParams(
            collective_id=0, has_side_effects=True, vmem_limit_bytes=60 * 2**20
        ),
    )(initial, measured, order, angle_index)


def solution(mesh):
    return jax.shard_map(
        functools.partial(on_device, mesh.shape["ray"], mesh.shape["cuts"]),
        mesh=mesh,
        in_specs=(P("cuts", "ray", None), P("ray", None, "cuts", None), P(), P()),
        out_specs=P("cuts", "ray", None),
        check_vma=False,
    )
```

```python
import functools

import jax
import jax.numpy as jnp
from jax import lax
from jax.experimental import pallas as pl
from jax.experimental.pallas import tpu as pltpu
from jax.sharding import PartitionSpec as P

SUBSETS = 2
NANG = 3000
TV_ITERS = 2
TV_STEP = 0.05
TV_EPS = 0.5
MESH = pl.DeviceIdType.MESH
LANE = 128


def split(value):
    high = value.astype(jnp.bfloat16)
    return high, (value - high.astype(jnp.float32)).astype(jnp.bfloat16)


dot = functools.partial(jnp.dot, preferred_element_type=jnp.float32)


def dot2(left, right):
    right_hi, right_lo = split(right)
    return dot(left, right_hi) + dot(left, right_lo)


def dot3(left_hi, left_lo, right):
    right_hi, right_lo = split(right)
    return dot(left_hi, right_hi) + dot(left_lo, right_hi) + dot(left_hi, right_lo)


def band_rows(rows, taps):
    half = rows // 2
    kept = []
    for group in range(-(-(rows + 1) // taps)):
        first = taps * group - half
        nearest = min(abs(first + j) for j in range(taps))
        ends = sum(1 for i in range(half) if half - 0.5 - i > nearest - 1)
        kept.append(min(half, -(-ends // 8) * 8))
    return kept


FAR_FIRST = (10, 11, 14, 15, 6, 7, 8, 9, 2, 3, 12, 13, 4, 5, 1)


def partner(me, mask):
    return sum(
        bit * (1 - (me // bit) % 2 if mask & bit else (me // bit) % 2) for bit in (1, 2, 4, 8)
    )


def chunk_of(ray):
    core, high, y = ray % 2, (ray // 2) % 2, ray // 4
    return 2 * (y + high * (7 - 2 * y)) + core


def ray_of(chunk):
    core, spot = chunk % 2, chunk // 2
    high = spot // 4
    y = spot + high * (7 - 2 * spot)
    return (y * 2 + high) * 2 + core


def kernel(
    rays, cuts,
    init_ref, meas_ref, order_in, angle_in, out_ref,
    order_ref, angle_ref, mv, m_mate, m_pick, xin, m_mid, m_all0, m_all1, m_edge, xw, kf, kb_hi, kb_lo,
    ext, pack, pland, hland, obuf,
    x_send, x_recv, t_send, t_recv, a_send, a_recv, z_send, z_recv, p_send, p_recv,
    h_send, h_recv, e_send, e_recv, o_send, o_recv, own_sem,
):
    slices, strip, breadth = init_ref.shape
    angles = meas_ref.shape[1]
    rows = strip * rays
    chunk = breadth // rays
    reach = chunk + 2 * LANE
    ring = chunk + LANE
    me = lax.axis_index("ray")
    cut = lax.axis_index("cuts")
    place = chunk_of(me)
    up, down = jnp.minimum(cut + 1, cuts - 1), jnp.maximum(cut - 1, 0)
    has_up, has_down = cut < cuts - 1, cut > 0
    sides = ((0, up, has_up, has_down), (1, down, has_down, has_up))
    east, west = ray_of(lax.rem(place + 1, rays)), ray_of(lax.rem(place + rays - 1, rays))
    peers = [partner(me, mask) for mask in FAR_FIRST]
    core, mate = me % 2, partner(me, 1)
    alike = [partner(me, mask) for mask in FAR_FIRST if mask % 2 == 0]
    m_all = (m_all0, m_all1)
    pairs = rays // 2

    barrier = pltpu.get_barrier_semaphore()
    for peer in peers:
        pl.semaphore_signal(barrier, inc=1, device_id=(peer, cut), device_id_type=MESH)
    for _, near, there, _ in sides:
        @pl.when(there)
        def _(near=near):
            pl.semaphore_signal(barrier, inc=1, device_id=(me, near), device_id_type=MESH)

    def window(spot):
        start = jnp.clip(spot * chunk - LANE, 0, breadth - reach)
        offset = start - spot * chunk + 2 * LANE
        return pl.multiple_of(start, LANE), pl.multiple_of(offset, LANE)

    local = [
        pltpu.make_async_copy(order_in, order_ref, own_sem.at[0]),
        pltpu.make_async_copy(angle_in, angle_ref, own_sem.at[1]),
    ]
    start, offset = window(place)
    mine = pltpu.make_async_copy(
        init_ref.at[:, :, pl.ds(start, reach)],
        xin.at[me, :, :, pl.ds(offset, reach)],
        own_sem.at[2],
    )
    held = [
        pltpu.make_async_copy(meas_ref.at[0, :, s], mv.at[s], own_sem.at[3 + s])
        for s in range(slices)
    ]
    for copy in [*local, *held, mine]:
        copy.start()

    def send(src, dst, send_sem, recv_sem, target):
        return pltpu.make_async_remote_copy(
            src_ref=src, dst_ref=dst, send_sem=send_sem, recv_sem=recv_sem,
            device_id=target, device_id_type=MESH,
        )

    def x_copy(peer, arriving):
        start, offset = window(place if arriving else chunk_of(peer))
        origin = peer if arriving else me
        return send(
            init_ref.at[:, :, pl.ds(start, reach)],
            xin.at[origin, :, :, pl.ds(offset, reach)],
            x_send.at[peer], x_recv.at[origin], (peer, cut),
        )

    def mate_copy(pair):
        theirs = pl.multiple_of(chunk * (2 * pair + 1 - core), chunk)
        return send(
            mv.at[:, :, pl.ds(theirs, chunk)], m_mate.at[pair],
            t_send.at[pair], t_recv.at[pair], (mate, cut),
        )

    def a_copy(subset, peer, arriving):
        origin = peer if arriving else me
        return send(
            m_pick.at[subset, (place if arriving else chunk_of(peer)) // 2],
            m_all[subset].at[origin // 2],
            a_send.at[subset, peer // 2], a_recv.at[subset, origin // 2], (peer, cut),
        )

    def o_copy(peer, arriving):
        column = pl.multiple_of(chunk * (chunk_of(peer) if arriving else place), chunk)
        origin = peer if arriving else me
        return send(
            obuf.at[peer], out_ref.at[:, :, pl.ds(column, chunk)],
            o_send.at[peer], o_recv.at[origin], (peer, cut),
        )

    def iota(shape, dim):
        return lax.broadcasted_iota(jnp.int32, shape, dim)

    half = rows // 2
    taps_f = kf.shape[2] // rows
    taps_b = kb_hi.shape[2] // angles
    bands = band_rows(rows, taps_b)

    def geometry(subset):
        slot = order_ref[subset]
        picked = angle_ref[pl.ds(slot, 1), :].astype(jnp.float32)
        slope_row = -1.0 + (2.0 * picked + 1.0) / NANG
        wide = jnp.broadcast_to(slope_row, (angles, angles))
        eye = iota((angles, angles), 0) == iota((angles, angles), 1)
        slope_col = jnp.sum(jnp.where(eye, wide, 0.0), axis=1, keepdims=True)
        lane = iota((angles, taps_f * rows), 1)
        position = (lane % rows).astype(jnp.float32) - (rows - 1) / 2.0
        spread = jnp.floor(slope_col * position * 256.0 + 0.5) / 256.0
        tap = lane // rows - half
        for group in range(kf.shape[1] // angles):
            reached = (tap + taps_f * group).astype(jnp.float32)
            hat = jnp.maximum(1.0 - jnp.abs(reached - spread), 0.0)
            kf[subset, group * angles:(group + 1) * angles, :] = hat.astype(jnp.bfloat16)
        slope_wide = jnp.concatenate([slope_row] * taps_b, axis=1)
        lane = iota((rows, taps_b * angles), 1)
        position = iota((rows, taps_b * angles), 0).astype(jnp.float32) - (rows - 1) / 2.0
        spread = slope_wide * position
        tap = lane // angles - half
        line = 0
        for group, ends in enumerate(bands):
            reached = (tap + taps_b * group).astype(jnp.float32)
            hat = jnp.maximum(1.0 - jnp.abs(reached - spread), 0.0)
            if 2 * ends < rows:
                hat = jnp.concatenate([hat[:ends], hat[rows - ends:]], axis=0)
            high, low = split(hat)
            kb_hi[subset, line:line + 2 * ends, :] = high
            kb_lo[subset, line:line + 2 * ends, :] = low
            line += 2 * ends

    for side, _, _, comes in sides:
        @pl.when(jnp.logical_not(comes))
        def _(side=side):
            for subset in range(SUBSETS):
                for s in range(slices):
                    ext[2 * subset, (2 + slices) * side + s] = jnp.zeros((rows, ring), jnp.float32)
                pland[subset, side] = jnp.zeros((8, LANE), jnp.float32)

    for copy in local:
        copy.wait()
    for subset in range(SUBSETS):
        geometry(subset)
    pl.semaphore_wait(barrier, rays - 1 + has_up.astype(jnp.int32) + has_down.astype(jnp.int32))

    for copy in held:
        copy.wait()
    spots = [chunk_of(peer) // 2 for peer in alike] + [place // 2]
    for pair in spots:
        mate_copy(pair).start()
    def hand_on(subset):
        ours = order_ref[subset] == me
        for pair, peer in zip(spots, [*alike, None]):
            if subset == 0:
                mate_copy(pair).wait_recv()
            column = pl.multiple_of(chunk * (2 * pair + core), chunk)
            picked = jnp.where(ours, mv[:, :, pl.ds(column, chunk)], m_mate[pair])
            if peer is None:
                m_all[subset][me // 2] = picked
            else:
                m_pick[subset, pair] = picked
                a_copy(subset, peer, False).start()

    for peer in peers:
        x_copy(peer, False).start()
    hand_on(0)

    start, offset = window(place)
    mine.wait()
    for peer in peers:
        x_copy(peer, True).wait_recv()

    column = iota((1, reach), 1) + place * chunk - LANE
    inside = (column >= 0) & (column < breadth)
    for s in range(slices):
        for p in range(rays):
            part = xin[p, s, :, LANE:LANE + reach]
            xw[s, p * strip:(p + 1) * strip, :] = jnp.where(inside, part, 0.0)

    half_lane = iota((1, LANE), 1) < LANE // 2

    def circle(value):
        edge = jnp.where(half_lane, value[:, reach - LANE:], value[:, :LANE])
        return jnp.concatenate([value[:, LANE:LANE + chunk], edge], axis=1)

    def turn(value, amount):
        amount = amount % value.shape[1]
        return value if amount == 0 else pltpu.roll(value, amount, 1)

    def project(subset, s):
        current = xw[s]
        stacked = jnp.concatenate([turn(current, j) for j in range(taps_f)], axis=0)
        lines = dot2(kf[subset], stacked)
        forward = jnp.zeros((angles, reach), jnp.float32)
        for group in range(kf.shape[1] // angles):
            forward += turn(lines[group * angles:(group + 1) * angles], taps_f * group - half)
        return forward

    def back_project(subset, s, forward, stored):
        residual = circle(jnp.where(inside, stored - forward, 0.0))
        stacked = jnp.concatenate([turn(residual, -j) for j in range(taps_b)], axis=0)
        lines = dot3(kb_hi[subset], kb_lo[subset], stacked)
        blocks = [jnp.zeros((8, ring), jnp.float32) for _ in range(rows // 8)]
        line = 0
        for group, ends in enumerate(bands):
            turned = turn(lines[line:line + 2 * ends], half - taps_b * group)
            line += 2 * ends
            for at in range(2 * ends // 8):
                row = at if at < ends // 8 else at + (rows - 2 * ends) // 8
                blocks[row] = blocks[row] + turned[at * 8:(at + 1) * 8]
        return circle(xw[s]) + jnp.concatenate(blocks, axis=0) / (rows * angles)

    lane = iota((1, ring), 1)
    ring_column = place * chunk + jnp.where(lane < chunk + LANE // 2, lane, lane - ring)
    valid_c = (ring_column >= 0) & (ring_column < breadth - 1)
    valid_r = iota((rows, 1), 0) < rows - 1
    first_slice = cut * slices - 2
    total_slices = slices * cuts

    def tv_pass(source, target, low, high, hand_sideways=False):
        before = None
        copies = []
        for t in range(low - 1, high):
            centre = ext[source, t]
            step_s = ext[source, t + 1] - centre
            at = first_slice + t
            step_s = jnp.where((at >= 0) & (at < total_slices - 1), step_s, 0.0)
            step_r = jnp.where(valid_r, pltpu.roll(centre, rows - 1, 0) - centre, 0.0)
            step_c = jnp.where(valid_c, turn(centre, -1) - centre, 0.0)
            inverse = lax.rsqrt(
                step_s * step_s + step_r * step_r + step_c * step_c + TV_EPS * TV_EPS
            )
            flow_s = step_s * inverse
            if t >= low:
                flow_r = step_r * inverse
                flow_c = step_c * inverse
                spread = flow_s - before
                spread = spread + flow_r - pltpu.roll(flow_r, 1, 0)
                spread = spread + flow_c - turn(flow_c, 1)
                ext[target, t] = centre + TV_STEP * spread
                if hand_sideways:
                    for side, near, at in ((0, east, chunk - LANE), (1, west, 0)):
                        copies.append(send(
                            ext.at[target, t, :, pl.ds(at, LANE)], hland.at[side, t - low],
                            h_send.at[side, t - low], h_recv.at[side, t - low], (near, cut),
                        ))
                        copies[-1].start()
            before = flow_s
        return copies

    def gather_measured(subset):
        for peer in alike:
            a_copy(subset, peer, True).wait_recv()
        m_mid[subset] = m_all[subset][order_ref[subset] // 2]
        copies = [
            send(
                m_mid.at[subset, :, :, pl.ds(at, LANE)], m_edge.at[subset, side],
                e_send.at[subset, side], e_recv.at[subset, side], (near, cut),
            )
            for side, near, at in ((0, east, chunk - LANE), (1, west, 0))
        ]
        for copy in copies:
            copy.start()
        return copies

    def z_copy(subset, side, s):
        return send(
            ext.at[2 * subset, 2 + s, :, pl.ds(0, chunk)],
            ext.at[2 * subset, (2 + slices) * side + s, :, pl.ds(0, chunk)],
            z_send.at[subset, side, s], z_recv.at[subset, side, s], (me, sides[side][1]),
        )

    def p_copy(subset, side):
        return send(
            pack.at[subset], pland.at[subset, side],
            p_send.at[subset, side], p_recv.at[subset, side], (me, sides[side][1]),
        )

    octets = rows // 8
    pack_lane = iota((1, LANE), 1) // 4

    ahead = [project(0, s) for s in range(slices)]
    for subset in range(SUBSETS):
        for s in range(slices):
            if subset == 0:
                forward = ahead[s]
            else:
                for copy in side_copies[2 * s:2 * s + 2]:
                    copy.wait()
                joined = jnp.concatenate(
                    [hland[0, s], ext[3, 2 + s, :, :chunk], hland[1, s]], axis=1
                )
                xw[s] = jnp.where(inside, joined, 0.0)
                forward = project(subset, s)
            if s == 0 and subset == 0:
                edge_copies = [gather_measured(subset)]
                hand_on(1)
            if s == 0:
                for copy in edge_copies[subset]:
                    copy.wait_recv()
            stored = jnp.concatenate(
                [m_edge[subset, 0, s], m_mid[subset, s], m_edge[subset, 1, s]], axis=1
            )
            ext[2 * subset, 2 + s] = back_project(subset, s, forward, stored)
            for side, _, there, _ in sides:
                @pl.when(there)
                def _(side=side, s=s):
                    z_copy(subset, side, s).start()
        packed = jnp.zeros((8, LANE), jnp.float32)
        for s in range(slices):
            for g in range(octets):
                k = octets * s + g
                edge = ext[2 * subset, 2 + s, g * 8:(g + 1) * 8, chunk:]
                packed = jnp.where(pack_lane == k, turn(edge, 2 + 4 * k), packed)
        pack[subset] = packed
        for side, _, there, _ in sides:
            @pl.when(there)
            def _(side=side):
                p_copy(subset, side).start()
        for side, _, there, comes in sides:
            @pl.when(comes)
            def _(side=side):
                for s in range(slices):
                    z_copy(subset, side, s).wait_recv()
                p_copy(subset, side).wait_recv()
            base = (2 + slices) * side
            packed = pland[subset, side]
            for s in range(slices):
                for g in range(octets):
                    k = octets * s + g
                    ext[2 * subset, base + s, g * 8:(g + 1) * 8, chunk:] = turn(packed, -(2 + 4 * k))
        tv_pass(2 * subset, 1, 1, 3 + slices)
        side_copies = tv_pass(1, 3, 2, 2 + slices, subset < SUBSETS - 1)
        if subset < SUBSETS - 1:
            edge_copies.append(gather_measured(subset + 1))
    for s in range(slices):
        for p in range(rays):
            obuf[p, s] = ext[3, 2 + s, p * strip:(p + 1) * strip, :chunk]
    for peer in peers:
        o_copy(peer, False).start()
    column = pl.multiple_of(place * chunk, chunk)
    last = pltpu.make_async_copy(obuf.at[me], out_ref.at[:, :, pl.ds(column, chunk)], own_sem.at[2])
    last.start()

    for peer in peers:
        x_copy(peer, False).wait_send()
    for pair in range(pairs):
        mate_copy(pair).wait_send()
    for subset in range(SUBSETS):
        for peer in alike:
            a_copy(subset, peer, False).wait_send()
    for copies in edge_copies:
        for copy in copies:
            copy.wait_send()
    for side, _, there, _ in sides:
        @pl.when(there)
        def _(side=side):
            for subset in range(SUBSETS):
                for s in range(slices):
                    z_copy(subset, side, s).wait_send()
                p_copy(subset, side).wait_send()


    for peer in peers:
        o_copy(peer, True).wait_recv()
    for peer in peers:
        o_copy(peer, False).wait_send()
    last.wait()


def pass_on(source, target, sem):
    copy = pltpu.make_async_copy(source, target, sem.at[0])
    copy.start()
    copy.wait()


def on_device(rays, cuts, initial, measured, order, angle_index):
    slices, strip, breadth = initial.shape
    angles = measured.shape[1]
    rows = strip * rays
    chunk = breadth // rays
    reach = chunk + 2 * LANE
    ring = chunk + LANE
    taps_f, taps_b = 4, 8
    groups_f = -(-(rows + 1) // taps_f)
    lines_b = 2 * sum(band_rows(rows, taps_b))
    dma = pltpu.SemaphoreType.DMA
    f32, bf16 = jnp.float32, jnp.bfloat16
    anywhere = pl.BlockSpec(memory_space=pl.ANY)

    gathered = pl.pallas_call(
        functools.partial(kernel, rays, cuts),
        out_shape=jax.ShapeDtypeStruct(initial.shape, f32),
        in_specs=[anywhere] * 4,
        out_specs=anywhere,
        scratch_shapes=[
            pltpu.SMEM(order.shape, jnp.int32),
            pltpu.VMEM(angle_index.shape, jnp.int32),
            pltpu.VMEM((slices, angles, breadth), f32),
            pltpu.VMEM((rays // 2, slices, angles, chunk), f32),
            pltpu.VMEM((SUBSETS, rays // 2, slices, angles, chunk), f32),
            pltpu.VMEM((rays, slices, strip, reach + 2 * LANE), f32),
            pltpu.VMEM((SUBSETS, slices, angles, chunk), f32),
            pltpu.VMEM((rays // 2, slices, angles, chunk), f32),
            pltpu.VMEM((rays // 2, slices, angles, chunk), f32),
            pltpu.VMEM((SUBSETS, 2, slices, angles, LANE), f32),
            pltpu.VMEM((slices, rows, reach), f32),
            pltpu.VMEM((SUBSETS, groups_f * angles, taps_f * rows), bf16),
            pltpu.VMEM((SUBSETS, lines_b, taps_b * angles), bf16),
            pltpu.VMEM((SUBSETS, lines_b, taps_b * angles), bf16),
            pltpu.VMEM((4, slices + 4, rows, ring), f32),
            pltpu.VMEM((SUBSETS, 8, LANE), f32),
            pltpu.VMEM((SUBSETS, 2, 8, LANE), f32),
            pltpu.VMEM((2, slices, rows, LANE), f32),
            pltpu.VMEM((rays, slices, strip, chunk), f32),
            dma((rays,)), dma((rays,)),
            dma((rays // 2,)), dma((rays // 2,)),
            dma((SUBSETS, rays // 2)), dma((SUBSETS, rays // 2)),
            dma((SUBSETS, 2, slices)), dma((SUBSETS, 2, slices)),
            dma((SUBSETS, 2)), dma((SUBSETS, 2)),
            dma((2, slices)), dma((2, slices)),
            dma((SUBSETS, 2)), dma((SUBSETS, 2)),
            dma((rays,)), dma((rays,)),
            dma((3 + slices,)),
        ],
        compiler_params=pltpu.CompilerParams(
            collective_id=0, has_side_effects=True, vmem_limit_bytes=60 * 2**20
        ),
    )(initial, measured, order, angle_index)
    return gathered


def solution(mesh):
    return jax.shard_map(
        functools.partial(on_device, mesh.shape["ray"], mesh.shape["cuts"]),
        mesh=mesh,
        in_specs=(P("cuts", "ray", None), P("ray", None, "cuts", None), P(), P()),
        out_specs=P("cuts", "ray", None),
        check_vma=False,
    )
```

```python
import functools

import jax
import jax.numpy as jnp
from jax import lax
from jax.experimental import pallas as pl
from jax.experimental.pallas import tpu as pltpu
from jax.sharding import PartitionSpec as P

SUBSETS = 2
NANG = 3000
TV_ITERS = 2
TV_STEP = 0.05
TV_EPS = 0.5
MESH = pl.DeviceIdType.MESH
LANE = 128


def split(value):
    high = value.astype(jnp.bfloat16)
    return high, (value - high.astype(jnp.float32)).astype(jnp.bfloat16)


dot = functools.partial(jnp.dot, preferred_element_type=jnp.float32)


def dot2(left, right):
    right_hi, right_lo = split(right)
    return dot(left, right_hi) + dot(left, right_lo)


def dot3(left_hi, left_lo, right):
    right_hi, right_lo = split(right)
    return dot(left_hi, right_hi) + dot(left_lo, right_hi) + dot(left_hi, right_lo)


def band_rows(rows, taps):
    half = rows // 2
    kept = []
    for group in range(-(-(rows + 1) // taps)):
        first = taps * group - half
        nearest = min(abs(first + j) for j in range(taps))
        ends = sum(1 for i in range(half) if half - 0.5 - i > nearest - 1)
        kept.append(min(half, -(-ends // 8) * 8))
    return kept


FAR_FIRST = (10, 11, 14, 15, 6, 7, 8, 9, 2, 3, 12, 13, 4, 5, 1)


def partner(me, mask):
    return sum(
        bit * (1 - (me // bit) % 2 if mask & bit else (me // bit) % 2) for bit in (1, 2, 4, 8)
    )


def chunk_of(ray):
    core, high, y = ray % 2, (ray // 2) % 2, ray // 4
    return 2 * (y + high * (7 - 2 * y)) + core


def ray_of(chunk):
    core, spot = chunk % 2, chunk // 2
    high = spot // 4
    y = spot + high * (7 - 2 * spot)
    return (y * 2 + high) * 2 + core


def kernel(
    rays, cuts,
    init_ref, meas_ref, order_in, angle_in, out_ref,
    order_ref, angle_ref, mv, m_mate, m_pick, xin, m_mid, m_all0, m_all1, m_edge, xw, kf, kb_hi, kb_lo,
    ext, pack, pland, hland, obuf,
    x_send, x_recv, t_send, t_recv, a_send, a_recv, z_send, z_recv, p_send, p_recv,
    h_send, h_recv, e_send, e_recv, o_send, o_recv, own_sem,
):
    slices, strip, breadth = init_ref.shape
    angles = meas_ref.shape[1]
    rows = strip * rays
    chunk = breadth // rays
    reach = chunk + 2 * LANE
    ring = chunk + LANE
    me = lax.axis_index("ray")
    cut = lax.axis_index("cuts")
    place = chunk_of(me)
    up, down = jnp.minimum(cut + 1, cuts - 1), jnp.maximum(cut - 1, 0)
    has_up, has_down = cut < cuts - 1, cut > 0
    sides = ((0, up, has_up, has_down), (1, down, has_down, has_up))
    east, west = ray_of(lax.rem(place + 1, rays)), ray_of(lax.rem(place + rays - 1, rays))
    peers = [partner(me, mask) for mask in FAR_FIRST]
    core, mate = me % 2, partner(me, 1)
    alike = [partner(me, mask) for mask in FAR_FIRST if mask % 2 == 0]
    m_all = (m_all0, m_all1)
    pairs = rays // 2

    barrier = pltpu.get_barrier_semaphore()
    for peer in peers:
        pl.semaphore_signal(barrier, inc=1, device_id=(peer, cut), device_id_type=MESH)
    for _, near, there, _ in sides:
        @pl.when(there)
        def _(near=near):
            pl.semaphore_signal(barrier, inc=1, device_id=(me, near), device_id_type=MESH)

    def window(spot):
        start = jnp.clip(spot * chunk - LANE, 0, breadth - reach)
        offset = start - spot * chunk + 2 * LANE
        return pl.multiple_of(start, LANE), pl.multiple_of(offset, LANE)

    local = [
        pltpu.make_async_copy(order_in, order_ref, own_sem.at[0]),
        pltpu.make_async_copy(angle_in, angle_ref, own_sem.at[1]),
    ]
    start, offset = window(place)
    mine = pltpu.make_async_copy(
        init_ref.at[:, :, pl.ds(start, reach)],
        xin.at[me, :, :, pl.ds(offset, reach)],
        own_sem.at[2],
    )
    held = [
        pltpu.make_async_copy(meas_ref.at[0, :, s], mv.at[s], own_sem.at[3 + s])
        for s in range(slices)
    ]
    for copy in [*local, *held, mine]:
        copy.start()

    def send(src, dst, send_sem, recv_sem, target):
        return pltpu.make_async_remote_copy(
            src_ref=src, dst_ref=dst, send_sem=send_sem, recv_sem=recv_sem,
            device_id=target, device_id_type=MESH,
        )

    def x_copy(peer, arriving):
        start, offset = window(place if arriving else chunk_of(peer))
        origin = peer if arriving else me
        return send(
            init_ref.at[:, :, pl.ds(start, reach)],
            xin.at[origin, :, :, pl.ds(offset, reach)],
            x_send.at[peer], x_recv.at[origin], (peer, cut),
        )

    def mate_copy(pair):
        theirs = pl.multiple_of(chunk * (2 * pair + 1 - core), chunk)
        return send(
            mv.at[:, :, pl.ds(theirs, chunk)], m_mate.at[pair],
            t_send.at[pair], t_recv.at[pair], (mate, cut),
        )

    def a_copy(subset, peer, arriving):
        origin = peer if arriving else me
        return send(
            m_pick.at[subset, (place if arriving else chunk_of(peer)) // 2],
            m_all[subset].at[origin // 2],
            a_send.at[subset, peer // 2], a_recv.at[subset, origin // 2], (peer, cut),
        )

    def o_copy(peer, arriving):
        column = pl.multiple_of(chunk * (chunk_of(peer) if arriving else place), chunk)
        origin = peer if arriving else me
        return send(
            obuf.at[peer], out_ref.at[:, :, pl.ds(column, chunk)],
            o_send.at[peer], o_recv.at[origin], (peer, cut),
        )

    def iota(shape, dim):
        return lax.broadcasted_iota(jnp.int32, shape, dim)

    half = rows // 2
    taps_f = kf.shape[2] // rows
    taps_b = kb_hi.shape[2] // angles
    bands = band_rows(rows, taps_b)

    def geometry(subset):
        slot = order_ref[subset]
        picked = angle_ref[pl.ds(slot, 1), :].astype(jnp.float32)
        slope_row = -1.0 + (2.0 * picked + 1.0) / NANG
        wide = jnp.broadcast_to(slope_row, (angles, angles))
        eye = iota((angles, angles), 0) == iota((angles, angles), 1)
        slope_col = jnp.sum(jnp.where(eye, wide, 0.0), axis=1, keepdims=True)
        lane = iota((angles, taps_f * rows), 1)
        position = (lane % rows).astype(jnp.float32) - (rows - 1) / 2.0
        spread = jnp.floor(slope_col * position * 256.0 + 0.5) / 256.0
        tap = lane // rows - half
        for group in range(kf.shape[1] // angles):
            reached = (tap + taps_f * group).astype(jnp.float32)
            hat = jnp.maximum(1.0 - jnp.abs(reached - spread), 0.0)
            kf[subset, group * angles:(group + 1) * angles, :] = hat.astype(jnp.bfloat16)
        slope_wide = jnp.concatenate([slope_row] * taps_b, axis=1)
        lane = iota((rows, taps_b * angles), 1)
        position = iota((rows, taps_b * angles), 0).astype(jnp.float32) - (rows - 1) / 2.0
        spread = slope_wide * position
        tap = lane // angles - half
        line = 0
        for group, ends in enumerate(bands):
            reached = (tap + taps_b * group).astype(jnp.float32)
            hat = jnp.maximum(1.0 - jnp.abs(reached - spread), 0.0)
            if 2 * ends < rows:
                hat = jnp.concatenate([hat[:ends], hat[rows - ends:]], axis=0)
            high, low = split(hat)
            kb_hi[subset, line:line + 2 * ends, :] = high
            kb_lo[subset, line:line + 2 * ends, :] = low
            line += 2 * ends

    for side, _, _, comes in sides:
        @pl.when(jnp.logical_not(comes))
        def _(side=side):
            for subset in range(SUBSETS):
                for s in range(slices):
                    ext[2 * subset, (2 + slices) * side + s] = jnp.zeros((rows, ring), jnp.float32)
                pland[subset, side] = jnp.zeros((8, LANE), jnp.float32)

    for copy in local:
        copy.wait()
    pl.semaphore_wait(barrier, rays - 1 + has_up.astype(jnp.int32) + has_down.astype(jnp.int32))

    for copy in held:
        copy.wait()
    spots = [chunk_of(peer) // 2 for peer in alike] + [place // 2]
    for pair in spots:
        mate_copy(pair).start()
    def hand_on(subset):
        ours = order_ref[subset] == me
        for pair, peer in zip(spots, [*alike, None]):
            if subset == 0:
                mate_copy(pair).wait_recv()
            column = pl.multiple_of(chunk * (2 * pair + core), chunk)
            picked = jnp.where(ours, mv[:, :, pl.ds(column, chunk)], m_mate[pair])
            if peer is None:
                m_all[subset][me // 2] = picked
            else:
                m_pick[subset, pair] = picked
                a_copy(subset, peer, False).start()

    for peer in peers:
        x_copy(peer, False).start()
    hand_on(0)
    for subset in range(SUBSETS):
        geometry(subset)

    start, offset = window(place)
    mine.wait()
    for peer in peers:
        x_copy(peer, True).wait_recv()

    column = iota((1, reach), 1) + place * chunk - LANE
    inside = (column >= 0) & (column < breadth)
    for s in range(slices):
        for p in range(rays):
            part = xin[p, s, :, LANE:LANE + reach]
            xw[s, p * strip:(p + 1) * strip, :] = jnp.where(inside, part, 0.0)

    half_lane = iota((1, LANE), 1) < LANE // 2

    def circle(value):
        edge = jnp.where(half_lane, value[:, reach - LANE:], value[:, :LANE])
        return jnp.concatenate([value[:, LANE:LANE + chunk], edge], axis=1)

    def turn(value, amount):
        amount = amount % value.shape[1]
        return value if amount == 0 else pltpu.roll(value, amount, 1)

    def project(subset, s):
        current = xw[s]
        stacked = jnp.concatenate([turn(current, j) for j in range(taps_f)], axis=0)
        lines = dot2(kf[subset], stacked)
        forward = jnp.zeros((angles, reach), jnp.float32)
        for group in range(kf.shape[1] // angles):
            forward += turn(lines[group * angles:(group + 1) * angles], taps_f * group - half)
        return forward

    def back_project(subset, s, forward, stored):
        residual = circle(jnp.where(inside, stored - forward, 0.0))
        stacked = jnp.concatenate([turn(residual, -j) for j in range(taps_b)], axis=0)
        lines = dot3(kb_hi[subset], kb_lo[subset], stacked)
        blocks = [jnp.zeros((8, ring), jnp.float32) for _ in range(rows // 8)]
        line = 0
        for group, ends in enumerate(bands):
            turned = turn(lines[line:line + 2 * ends], half - taps_b * group)
            line += 2 * ends
            for at in range(2 * ends // 8):
                row = at if at < ends // 8 else at + (rows - 2 * ends) // 8
                blocks[row] = blocks[row] + turned[at * 8:(at + 1) * 8]
        return circle(xw[s]) + jnp.concatenate(blocks, axis=0) / (rows * angles)

    lane = iota((1, ring), 1)
    ring_column = place * chunk + jnp.where(lane < chunk + LANE // 2, lane, lane - ring)
    valid_c = (ring_column >= 0) & (ring_column < breadth - 1)
    valid_r = iota((rows, 1), 0) < rows - 1
    first_slice = cut * slices - 2
    total_slices = slices * cuts

    def tv_pass(source, target, low, high, hand_sideways=False):
        before = None
        copies = []
        for t in range(low - 1, high):
            centre = ext[source, t]
            step_s = ext[source, t + 1] - centre
            at = first_slice + t
            step_s = jnp.where((at >= 0) & (at < total_slices - 1), step_s, 0.0)
            step_r = jnp.where(valid_r, pltpu.roll(centre, rows - 1, 0) - centre, 0.0)
            step_c = jnp.where(valid_c, turn(centre, -1) - centre, 0.0)
            inverse = lax.rsqrt(
                step_s * step_s + step_r * step_r + step_c * step_c + TV_EPS * TV_EPS
            )
            flow_s = step_s * inverse
            if t >= low:
                flow_r = step_r * inverse
                flow_c = step_c * inverse
                spread = flow_s - before
                spread = spread + flow_r - pltpu.roll(flow_r, 1, 0)
                spread = spread + flow_c - turn(flow_c, 1)
                ext[target, t] = centre + TV_STEP * spread
                if hand_sideways:
                    for side, near, at in ((0, east, chunk - LANE), (1, west, 0)):
                        copies.append(send(
                            ext.at[target, t, :, pl.ds(at, LANE)], hland.at[side, t - low],
                            h_send.at[side, t - low], h_recv.at[side, t - low], (near, cut),
                        ))
                        copies[-1].start()
            before = flow_s
        return copies

    def gather_measured(subset):
        for peer in alike:
            a_copy(subset, peer, True).wait_recv()
        m_mid[subset] = m_all[subset][order_ref[subset] // 2]
        copies = [
            send(
                m_mid.at[subset, :, :, pl.ds(at, LANE)], m_edge.at[subset, side],
                e_send.at[subset, side], e_recv.at[subset, side], (near, cut),
            )
            for side, near, at in ((0, east, chunk - LANE), (1, west, 0))
        ]
        for copy in copies:
            copy.start()
        return copies

    def z_copy(subset, side, s):
        return send(
            ext.at[2 * subset, 2 + s, :, pl.ds(0, chunk)],
            ext.at[2 * subset, (2 + slices) * side + s, :, pl.ds(0, chunk)],
            z_send.at[subset, side, s], z_recv.at[subset, side, s], (me, sides[side][1]),
        )

    def p_copy(subset, side):
        return send(
            pack.at[subset], pland.at[subset, side],
            p_send.at[subset, side], p_recv.at[subset, side], (me, sides[side][1]),
        )

    octets = rows // 8
    pack_lane = iota((1, LANE), 1) // 4

    ahead = [project(0, s) for s in range(slices)]
    for subset in range(SUBSETS):
        for s in range(slices):
            if subset == 0:
                forward = ahead[s]
            else:
                for copy in side_copies[2 * s:2 * s + 2]:
                    copy.wait()
                joined = jnp.concatenate(
                    [hland[0, s], ext[3, 2 + s, :, :chunk], hland[1, s]], axis=1
                )
                xw[s] = jnp.where(inside, joined, 0.0)
                forward = project(subset, s)
            if s == 0 and subset == 0:
                edge_copies = [gather_measured(subset)]
                hand_on(1)
            if s == 0:
                for copy in edge_copies[subset]:
                    copy.wait_recv()
            stored = jnp.concatenate(
                [m_edge[subset, 0, s], m_mid[subset, s], m_edge[subset, 1, s]], axis=1
            )
            ext[2 * subset, 2 + s] = back_project(subset, s, forward, stored)
            for side, _, there, _ in sides:
                @pl.when(there)
                def _(side=side, s=s):
                    z_copy(subset, side, s).start()
        packed = jnp.zeros((8, LANE), jnp.float32)
        for s in range(slices):
            for g in range(octets):
                k = octets * s + g
                edge = ext[2 * subset, 2 + s, g * 8:(g + 1) * 8, chunk:]
                packed = jnp.where(pack_lane == k, turn(edge, 2 + 4 * k), packed)
        pack[subset] = packed
        for side, _, there, _ in sides:
            @pl.when(there)
            def _(side=side):
                p_copy(subset, side).start()
        for side, _, there, comes in sides:
            @pl.when(comes)
            def _(side=side):
                for s in range(slices):
                    z_copy(subset, side, s).wait_recv()
                p_copy(subset, side).wait_recv()
            base = (2 + slices) * side
            packed = pland[subset, side]
            for s in range(slices):
                for g in range(octets):
                    k = octets * s + g
                    ext[2 * subset, base + s, g * 8:(g + 1) * 8, chunk:] = turn(packed, -(2 + 4 * k))
        tv_pass(2 * subset, 1, 1, 3 + slices)
        side_copies = tv_pass(1, 3, 2, 2 + slices, subset < SUBSETS - 1)
        if subset < SUBSETS - 1:
            edge_copies.append(gather_measured(subset + 1))
    for s in range(slices):
        for p in range(rays):
            obuf[p, s] = ext[3, 2 + s, p * strip:(p + 1) * strip, :chunk]
    for peer in peers:
        o_copy(peer, False).start()
    column = pl.multiple_of(place * chunk, chunk)
    last = pltpu.make_async_copy(obuf.at[me], out_ref.at[:, :, pl.ds(column, chunk)], own_sem.at[2])
    last.start()

    for peer in peers:
        x_copy(peer, False).wait_send()
    for pair in range(pairs):
        mate_copy(pair).wait_send()
    for subset in range(SUBSETS):
        for peer in alike:
            a_copy(subset, peer, False).wait_send()
    for copies in edge_copies:
        for copy in copies:
            copy.wait_send()
    for side, _, there, _ in sides:
        @pl.when(there)
        def _(side=side):
            for subset in range(SUBSETS):
                for s in range(slices):
                    z_copy(subset, side, s).wait_send()
                p_copy(subset, side).wait_send()


    for peer in peers:
        o_copy(peer, True).wait_recv()
    for peer in peers:
        o_copy(peer, False).wait_send()
    last.wait()


def pass_on(source, target, sem):
    copy = pltpu.make_async_copy(source, target, sem.at[0])
    copy.start()
    copy.wait()


def on_device(rays, cuts, initial, measured, order, angle_index):
    slices, strip, breadth = initial.shape
    angles = measured.shape[1]
    rows = strip * rays
    chunk = breadth // rays
    reach = chunk + 2 * LANE
    ring = chunk + LANE
    taps_f, taps_b = 4, 8
    groups_f = -(-(rows + 1) // taps_f)
    lines_b = 2 * sum(band_rows(rows, taps_b))
    dma = pltpu.SemaphoreType.DMA
    f32, bf16 = jnp.float32, jnp.bfloat16
    anywhere = pl.BlockSpec(memory_space=pl.ANY)

    gathered = pl.pallas_call(
        functools.partial(kernel, rays, cuts),
        out_shape=jax.ShapeDtypeStruct(initial.shape, f32),
        in_specs=[anywhere] * 4,
        out_specs=anywhere,
        scratch_shapes=[
            pltpu.SMEM(order.shape, jnp.int32),
            pltpu.VMEM(angle_index.shape, jnp.int32),
            pltpu.VMEM((slices, angles, breadth), f32),
            pltpu.VMEM((rays // 2, slices, angles, chunk), f32),
            pltpu.VMEM((SUBSETS, rays // 2, slices, angles, chunk), f32),
            pltpu.VMEM((rays, slices, strip, reach + 2 * LANE), f32),
            pltpu.VMEM((SUBSETS, slices, angles, chunk), f32),
            pltpu.VMEM((rays // 2, slices, angles, chunk), f32),
            pltpu.VMEM((rays // 2, slices, angles, chunk), f32),
            pltpu.VMEM((SUBSETS, 2, slices, angles, LANE), f32),
            pltpu.VMEM((slices, rows, reach), f32),
            pltpu.VMEM((SUBSETS, groups_f * angles, taps_f * rows), bf16),
            pltpu.VMEM((SUBSETS, lines_b, taps_b * angles), bf16),
            pltpu.VMEM((SUBSETS, lines_b, taps_b * angles), bf16),
            pltpu.VMEM((4, slices + 4, rows, ring), f32),
            pltpu.VMEM((SUBSETS, 8, LANE), f32),
            pltpu.VMEM((SUBSETS, 2, 8, LANE), f32),
            pltpu.VMEM((2, slices, rows, LANE), f32),
            pltpu.VMEM((rays, slices, strip, chunk), f32),
            dma((rays,)), dma((rays,)),
            dma((rays // 2,)), dma((rays // 2,)),
            dma((SUBSETS, rays // 2)), dma((SUBSETS, rays // 2)),
            dma((SUBSETS, 2, slices)), dma((SUBSETS, 2, slices)),
            dma((SUBSETS, 2)), dma((SUBSETS, 2)),
            dma((2, slices)), dma((2, slices)),
            dma((SUBSETS, 2)), dma((SUBSETS, 2)),
            dma((rays,)), dma((rays,)),
            dma((3 + slices,)),
        ],
        compiler_params=pltpu.CompilerParams(
            collective_id=0, has_side_effects=True, vmem_limit_bytes=60 * 2**20
        ),
    )(initial, measured, order, angle_index)
    return gathered


def solution(mesh):
    return jax.shard_map(
        functools.partial(on_device, mesh.shape["ray"], mesh.shape["cuts"]),
        mesh=mesh,
        in_specs=(P("cuts", "ray", None), P("ray", None, "cuts", None), P(), P()),
        out_specs=P("cuts", "ray", None),
        check_vma=False,
    )
```
